512 devices in a mesh: sweep: 32 (over x, y), cross: 16 (over z, core).
Axes of the slice: x: 4, y: 8, z: 8, core: 2. Of those that a mesh axis runs over, the one named last changes fastest.
Arguments:
- source: bfloat16 [128, 32, 1, 135, 256], P('sweep', 'cross'), may hold values from -0.23925781 to 0.23925781
- inv_diag: bfloat16 [128, 32, 1, 135, 135], P('sweep', 'cross'), may hold values from -0.0801 to 1.602
- upstream: bfloat16 [128, 32, 1, 135, 135], P('sweep', 'cross'), may hold values from -1.25 to 0.125
- downstream: bfloat16 [128, 32, 1, 135, 135], P('sweep', 'cross'), may hold values from -0.125 to 1.25
- cross_lower: bfloat16 [128, 32, 1, 135, 135], P('sweep', 'cross'), may hold values from -0.25 to 0.25
- cross_upper: bfloat16 [128, 32, 1, 135, 135], P('sweep', 'cross'), may hold values from -0.25 to 0.25
Outputs:
- update: float32 [128, 32, 1, 135, 256], P('sweep', 'cross')
The draws below stay inside these ranges and needn't reach their ends.
All inputs are finite; a program needn't handle non-finite values.
Results may differ from the reference program's by a relative error of at most 0.0003.
Values sent between devices are 32-bit elements; how exact they have to be, the bound alone decides.
No kernel may reach another device: no remote copies, remote signals or barrier semaphores. Data moves between devices by JAX's collectives and lax.ppermute only.
A program may use at most 128 MiB of HBM per device.

```python
import math
import jax
import jax.numpy as jnp
from jax import lax

BLOCK = 135
ELEMENT_PLANES = 1
RHS = 256
FLOW_ELEMENTS = 128
CROSS_ELEMENTS = 32


def coupling_parts(key):
    noise_key = jax.random.fold_in(key, 0)
    scale_key = jax.random.fold_in(key, 2)
    full_shape = (FLOW_ELEMENTS, CROSS_ELEMENTS, ELEMENT_PLANES, BLOCK, BLOCK)
    normal = jax.random.normal(noise_key, full_shape, jnp.float32)
    noise_part = normal
    unit_matrix = jnp.eye(BLOCK, dtype=jnp.float32)
    entries = jnp.clip(noise_part * (0.3 / math.sqrt(BLOCK)), -0.08, 0.08) * (1.0 - unit_matrix)
    scales = jnp.exp(jax.random.uniform(scale_key, full_shape[:4], jnp.float32, math.log(0.8), math.log(1.6)))
    return (entries, scales)


def chain_rates(key, slow_least, slow_most, slow_percent):
    mask_key, slow_key, fast_key, location_key, loss_key = jax.random.split(key, 5)
    grid_shape = (FLOW_ELEMENTS, CROSS_ELEMENTS, ELEMENT_PLANES, BLOCK)
    slow_mask = jax.random.randint(mask_key, (CROSS_ELEMENTS, ELEMENT_PLANES, BLOCK), 0, 100) < slow_percent
    slow_decay = jnp.exp(jax.random.uniform(slow_key, grid_shape, jnp.float32, math.log(slow_least), math.log(slow_most))) / FLOW_ELEMENTS
    fast_decay = jnp.exp(jax.random.uniform(fast_key, grid_shape, jnp.float32, math.log(0.06), math.log(0.2)))
    decays = jnp.where(slow_mask[None], slow_decay, fast_decay)
    sparse_locations = jax.random.randint(location_key, (2, CROSS_ELEMENTS, ELEMENT_PLANES), 0, FLOW_ELEMENTS)
    element_locations = jnp.arange(FLOW_ELEMENTS)[:, None, None]
    selected_entries = (element_locations == sparse_locations[0][None]) | (element_locations == sparse_locations[1][None])
    losses = jax.random.uniform(loss_key, (FLOW_ELEMENTS, CROSS_ELEMENTS, ELEMENT_PLANES), jnp.float32, 0.5, 0.8)
    factor = jnp.where(selected_entries, losses, 1.0)
    return jnp.exp(-decays) * factor[..., None]


def face_matrix(entries, scales, rates, polarity):
    inverse = 1.0 / scales
    weights = rates * inverse
    unit_matrix = jnp.eye(BLOCK, dtype=jnp.float32)
    matrix = weights[..., None] * unit_matrix - entries * inverse[..., :, None] * weights[..., None, :]
    return (polarity * matrix).astype(jnp.bfloat16)


def draw_inv_diag(key, part):
    entries, scales = coupling_parts(key)
    unit_matrix = jnp.eye(BLOCK, dtype=jnp.float32)
    return (entries + scales[..., None] * unit_matrix).astype(jnp.bfloat16)


def draw_upstream(key, part):
    slow_percent = 50
    entries, scales = coupling_parts(key)
    key = jax.random.fold_in(key, 23)
    rates = chain_rates(key, 0.25, 1.0, slow_percent)
    return face_matrix(entries, scales, rates, -1.0)


def draw_downstream(key, part):
    slow_percent = 50
    entries, scales = coupling_parts(key)
    key = jax.random.fold_in(key, 37)
    rates = chain_rates(key, 0.4, 1.2, slow_percent)
    return face_matrix(entries, scales, rates, 1.0)


def block_levels(rng, dims, cuts, low, top_value):
    level = 1.0
    for dim, parts in cuts:
        draws = jax.random.uniform(jax.random.fold_in(jax.random.fold_in(rng, 6), dim), (parts,), jnp.float32, low / len(cuts), top_value / len(cuts))
        level = level * jnp.repeat(jnp.exp(draws), dims[dim] // parts).reshape((-1,) + (1,) * (len(dims) - 1 - dim))
    return level


def scatter_about(key, shape, width, limit, shards=(), kind=jnp.bfloat16):
    values = jax.random.normal(key, shape, jnp.float32) * width
    if len(shards) > 0:
        values = block_levels(key, shape, shards, -0.22, 0.18) * values
    return jnp.clip(values, min=-limit, max=limit).astype(kind)


def setup_inputs(seed: int = 0) -> dict:
    splits = jax.random.split(jax.random.key(seed), 7)
    return {
        "source": scatter_about(splits[0], (FLOW_ELEMENTS, CROSS_ELEMENTS, ELEMENT_PLANES, BLOCK, RHS), 0.04, 0.23925781, ((0, 32), (1, 16))),
        "inv_diag": draw_inv_diag(jax.random.fold_in(splits[6], 71), 0),
        "upstream": draw_upstream(jax.random.fold_in(splits[6], 71), 0),
        "downstream": draw_downstream(jax.random.fold_in(splits[6], 71), 0),
        "cross_lower": scatter_about(splits[4], (FLOW_ELEMENTS, CROSS_ELEMENTS, ELEMENT_PLANES, BLOCK, BLOCK), (4 * BLOCK) ** -0.5, 0.25, ((0, 32), (1, 16))),
        "cross_upper": scatter_about(splits[5], (FLOW_ELEMENTS, CROSS_ELEMENTS, ELEMENT_PLANES, BLOCK, BLOCK), (4 * BLOCK) ** -0.5, 0.25, ((0, 32), (1, 16))),
    }


def apply_block(matrix, vector):
    return jnp.einsum("cpij,cpjr->cpir", matrix.astype(jnp.float32), vector.astype(jnp.float32), precision=lax.Precision.HIGHEST)


def reference(source, inv_diag, upstream, downstream, cross_lower, cross_upper):
    anchor = jnp.zeros(source.shape[1:], jnp.float32)

    def forward_step(previous, position):
        partial_value = source[position].astype(jnp.float32) - apply_block(upstream[position], previous)
        result = apply_block(inv_diag[position], partial_value)
        return result, result

    element_locations = jnp.arange(FLOW_ELEMENTS).astype(jnp.int32)
    ending, forward = lax.scan(forward_step, anchor, element_locations)
    border = jnp.zeros(source.shape[2:], jnp.float32)[None]

    def backward_step(following, position):
        before = jnp.maximum(position - 1, 0)
        previous = forward[before] * (position > 0).astype(jnp.float32)
        current = forward[position]
        lower_rim = jnp.concatenate([border, current[:-1]], axis=0)
        upper_rim = jnp.concatenate([current[1:], border], axis=0)
        balance = source[position].astype(jnp.float32) - apply_block(upstream[position], previous)
        balance = balance - apply_block(cross_lower[position], lower_rim) - apply_block(cross_upper[position], upper_rim)
        balance = balance - apply_block(downstream[position], following)
        result = apply_block(inv_diag[position], balance)
        return result, result

    beginning, update = lax.scan(backward_step, anchor, element_locations, reverse=True)
    return update
```

```python
import functools

import jax
import jax.numpy as jnp
from jax import lax
from jax.experimental import pallas as pl
from jax.experimental.pallas import tpu as pltpu
from jax.sharding import PartitionSpec as P

ROW = 8
LANES = 128
F32 = jnp.float32
BF16 = jnp.bfloat16


def halves(x):
    high = x.astype(BF16)
    return high, (x - high.astype(F32)).astype(BF16)


def mul(a, b):
    return jnp.dot(a, b, preferred_element_type=F32)


def exact_by_float(a, b):
    high, low = halves(b)
    return mul(a, high) + mul(a, low)


def float_by_float(a, b):
    a_high, a_low = halves(a)
    b_high, b_low = halves(b)
    return mul(a_high, b_high) + (mul(a_high, b_low) + mul(a_low, b_high))


def lane(shape):
    return lax.broadcasted_iota(jnp.int32, shape, len(shape) - 1)


def put(ref, at, value):
    rows = value.shape[0]
    full = ref.shape[-2]
    tail = full - full % 8 if full % 8 else full - 8
    ref[(*at, slice(tail, full), slice(None))] = jnp.zeros((full - tail, ref.shape[-1]), F32)
    ref[(*at, slice(0, rows), slice(0, value.shape[1]))] = value


def pack_map(matrix):
    rows = matrix.shape[0]
    strip = jnp.where(lane((rows, LANES)) < 8, matrix[:, LANES:], 0.0)
    folded = strip[:8]
    for t in range(1, 16):
        folded = folded + pltpu.roll(strip[8 * t : 8 * t + 8], 8 * t, 1)
    return jnp.concatenate([matrix[:, :LANES], folded, strip[128:]], axis=0)


def unpack_map(block):
    rows = block.shape[0] - 16
    folded = block[rows : rows + 8]
    parts = [folded] + [pltpu.roll(folded, LANES - 8 * t, 1) for t in range(1, 16)]
    strip = jnp.concatenate(parts + [block[rows + 8 :]], axis=0)
    strip = jnp.where(lane(strip.shape) < 8, strip, 0.0)
    return jnp.concatenate([block[:rows], strip], axis=1)


def fold_rows(low, high):
    top = (low.shape[0] // 8 + 1) // 2 * 8
    under = jnp.concatenate(
        [high[top:], jnp.zeros((2 * top - high.shape[0], LANES), F32)], axis=0
    )
    return jnp.where(lane((top, LANES)) < 64, low[:top], under)


def pack_slice(pair, odd):
    turned = pltpu.roll(pair, 64, 1)
    return fold_rows(turned, pair) if odd else fold_rows(pair, turned)


def unpack_slice(block, rows, odd):
    turned = pltpu.roll(block, 64, 1)
    first, second = (turned, block) if odd else (block, turned)
    both = jnp.concatenate([first, second[: rows - block.shape[0]]], axis=0)
    keep = lane(both.shape) >= 64 if odd else lane(both.shape) < 64
    return jnp.where(keep, both, 0.0)


def prepare(inverse, before, after, source, sent, fore_maps, fore_values, back_maps, back_steps):
    positions, columns, unknowns, vectors = source.shape
    full = fore_maps.shape[-2]
    last = positions - 1
    for s in range(positions):
        for c in range(columns):
            diagonal = inverse[s, c]
            step = -mul(diagonal, before[s, c])
            value = mul(diagonal, source[s, c])
            back_steps[s, c] = jnp.zeros((full, 2 * LANES), F32)
            put(back_steps, (s, c), -mul(diagonal, after[s, c]))
            if s == 0:
                fore_maps[s, c] = jnp.zeros((full, 2 * LANES), F32)
                put(fore_maps, (s, c), step)
                put(fore_values, (s, c), value)
            else:
                put(fore_maps, (s, c), float_by_float(step, fore_maps[s - 1, c, :unknowns]))
                put(
                    fore_values,
                    (s, c),
                    value + float_by_float(step, fore_values[s - 1, c, :unknowns]),
                )
    for c in range(columns):
        back_maps[last, c] = back_steps[last, c]
    for s in range(last - 1, -1, -1):
        for c in range(columns):
            back_maps[s, c] = float_by_float(back_steps[s, c, :, :full], back_maps[s + 1, c])
    peers = ROW // columns
    room = full + 16
    for c in range(columns):
        fore = pack_map(fore_maps[last, c])
        back = pack_map(back_maps[0, c])
        for q in range(peers):
            at = c * peers + q
            sent[at, 0:room] = fore
            sent[at, room : 2 * room] = back
            pair = fore_values[last, c, :, q // 2 * LANES : (q // 2 + 1) * LANES]
            sent[at, 2 * room :] = pack_slice(pair, q % 2)


def scan_maps(full, offset, order, received, states, maps=None):
    room = full + 16
    state = None
    for k, d in enumerate(order):
        matrix = unpack_map(received[d, offset : offset + room])
        if maps is not None:
            maps[k] = matrix
        state = matrix if state is None else float_by_float(matrix[:, :full], state)
        states[k] = state


def ship_row(full, state, sent):
    block = jnp.concatenate([pack_map(state), pack_slice(state[:, LANES:], 1)], axis=0)
    for x in range(sent.shape[0]):
        sent[x] = block


def fore_scan(full, received, states, sent):
    room = full + 16
    state = None
    for d in range(ROW):
        matrix = unpack_map(received[d, 0:room])
        value = unpack_slice(received[d, 2 * room :], full, 1)
        value = jnp.concatenate([jnp.zeros_like(value), value], axis=1)
        if state is None:
            state = matrix + value
        else:
            state = float_by_float(matrix[:, :full], state) + value
        states[d] = state
    ship_row(full, state, sent)


def back_scan(full, maps, products, received, states, sent):
    value = None
    for k in range(ROW):
        piece = unpack_slice(received[ROW - 1 - k], full, 1)
        if value is None:
            value = piece
        else:
            high, low = halves(maps[k][:, :full])
            v_high = value.astype(BF16).astype(F32)
            both = (v_high + pltpu.roll(value - v_high, 64, 1)).astype(BF16)
            first = mul(high, both)
            rest = pltpu.roll(first, 64, 1) + mul(low, v_high.astype(BF16))
            value = jnp.where(lane(first.shape) >= 64, first + rest, 0.0) + piece
        state = products[k]
        state = jnp.concatenate([state[:, :LANES], state[:, LANES:] + value], axis=1)
        states[k] = state
        if k == ROW - 1:
            ship_row(full, state, sent)


def enter(full, backward, row, received, states, sent):
    rows = received.shape[0]
    room = full + 16
    order = list(range(rows - 1, 0, -1)) if backward else list(range(rows - 1))
    mine = row[0]
    value = None
    found = jnp.zeros((full, LANES), F32)
    for x in order:
        piece = unpack_slice(received[x, room:], full, 0)
        if value is not None:
            matrix = unpack_map(received[x, 0:room])
            piece = float_by_float(matrix[:, :full], value) + piece
        value = piece
        found = jnp.where(mine == (x - 1 if backward else x + 1), value, found)
    high = found.astype(BF16).astype(F32)
    low = found - high
    under = jnp.zeros((2 * LANES - 64 - full, LANES), F32)
    corner = (
        lax.broadcasted_iota(jnp.int32, (64, LANES), 0) == lane((64, LANES))
    ).astype(F32)
    top = jnp.concatenate([high, under, corner], axis=0)
    bottom = jnp.concatenate([low, under, jnp.zeros((64, LANES), F32)], axis=0)
    both = (top + pltpu.roll(bottom, 64, 1)).astype(BF16)
    stack = states[0 : ROW - 1].reshape((ROW - 1) * full, 2 * LANES)
    s_high, s_low = halves(stack)
    first = mul(s_high, both)
    every = first + (pltpu.roll(first, 64, 1) + mul(s_low, top.astype(BF16)))
    sent[ROW - 1 if backward else 0] = pack_slice(found, 0)
    for k in range(ROW - 1):
        at = ROW - 2 - k if backward else k + 1
        sent[at] = pack_slice(every[k * full : (k + 1) * full], 0)


def gather_columns(full, received, c, columns):
    peers = ROW // columns
    parts = []
    for h in range(peers // 2):
        at = c * peers + 2 * h
        parts.append(
            unpack_slice(received[at], full, 0)
            + pltpu.roll(unpack_slice(received[at + 1], full, 0), 64, 1)
        )
    return jnp.concatenate(parts, axis=1)


def spread(received, maps, base, *outs):
    positions, columns, full, vectors = base.shape
    for c in range(columns):
        entering = gather_columns(full, received, c, columns)
        stack = jnp.concatenate([maps[s, c, :, :full] for s in range(positions)], axis=0)
        product = float_by_float(stack, entering)
        for s in range(positions):
            value = product[s * full : (s + 1) * full] + base[s, c]
            if len(outs) == 1:
                rows = outs[0].shape[-2]
                outs[0][s, c] = value[:rows]
            else:
                outs[c][s] = value


def own_part(inverse, lower, upper, head, tail, own):
    positions, columns, unknowns, _ = inverse.shape
    forward = (head, tail)
    for s in range(positions):
        for c in range(columns):
            value = forward[c][s]
            near = upper[s, c] if c == 0 else lower[s, c]
            drop = exact_by_float(near, forward[1 - c][s, :unknowns])
            put(own, (s, c), value[:unknowns] - exact_by_float(inverse[s, c], drop))


def back_part(inverse, lower, upper, below, above, steps, own, values, sent):
    positions, columns, unknowns, _ = inverse.shape
    full = own.shape[-2]
    halo = (below, above)
    for s in range(positions - 1, -1, -1):
        for c in range(columns):
            far = lower[s, c] if c == 0 else upper[s, c]
            drop = exact_by_float(far, halo[c][s, :unknowns])
            put(values, (s, c), own[s, c, :unknowns] - exact_by_float(inverse[s, c], drop))
            if s < positions - 1:
                values[s, c] += float_by_float(steps[s, c, :, :full], values[s + 1, c])
    peers = ROW // columns
    for c in range(columns):
        for q in range(peers):
            pair = values[0, c, :, q // 2 * LANES : (q // 2 + 1) * LANES]
            sent[c * peers + q] = pack_slice(pair, q % 2)


def call(kernel, outs, *args, flops=10**8, smem=()):
    vmem = pl.BlockSpec(memory_space=pltpu.VMEM)
    moved = sum(a.size * a.dtype.itemsize for a in args)
    return pl.pallas_call(
        kernel,
        out_shape=[jax.ShapeDtypeStruct(shape, F32) for shape in outs],
        in_specs=[
            pl.BlockSpec(memory_space=pltpu.SMEM) if i in smem else vmem for i in range(len(args))
        ],
        out_specs=[vmem] * len(outs),
        compiler_params=pltpu.CompilerParams(vmem_limit_bytes=28 * 2**20),
        cost_estimate=pl.CostEstimate(flops=flops, bytes_accessed=moved, transcendentals=0),
    )(*args)


def shards(source, inv_diag, upstream, downstream, cross_lower, cross_upper):
    positions, columns, planes, unknowns, vectors = source.shape
    squeeze = lambda a: a.reshape(positions, columns, *a.shape[3:])
    source, inverse, before = squeeze(source), squeeze(inv_diag), squeeze(upstream)
    after, lower, upper = squeeze(downstream), squeeze(cross_lower), squeeze(cross_upper)
    full = -(-unknowns // 8) * 8
    room = full + 16
    fold = (full // 8 + 1) // 2 * 8
    count = lax.axis_size("sweep")
    rows = count // ROW
    inside = [[r * ROW + i for i in range(ROW)] for r in range(rows)]
    across = [[r * ROW + i for r in range(rows)] for i in range(ROW)]
    row = (lax.axis_index("sweep") // ROW).astype(jnp.int32).reshape(1)
    block = (positions, columns, full, 2 * LANES)

    def exchange(x, groups):
        return lax.all_to_all(x, "sweep", 0, 0, axis_index_groups=groups)

    sent, fore_maps, fore_values, back_maps, back_steps = call(
        prepare,
        [(ROW, 2 * room + fold, LANES), block, block, block, block],
        inverse,
        before,
        after,
        source,
    )
    received = exchange(sent, inside)
    states, sent = call(
        functools.partial(fore_scan, full),
        [(ROW, full, 2 * LANES), (rows, room + fold, LANES)],
        received,
    )
    joined = exchange(sent, across)
    (sent,) = call(
        functools.partial(enter, full, False),
        [(ROW, fold, LANES)],
        row,
        joined,
        states,
        smem=(0,),
    )
    entering = exchange(sent, inside)
    head, tail = call(
        spread, [(positions, full, vectors)] * 2, entering, fore_maps, fore_values
    )
    ends = lax.axis_size("cross") - 1
    below = lax.ppermute(tail, "cross", [(i, i + 1) for i in range(ends)])
    above = lax.ppermute(head, "cross", [(i + 1, i) for i in range(ends)])
    (own,) = call(own_part, [block], inverse, lower, upper, head, tail)
    products, maps = call(
        functools.partial(scan_maps, full, room, range(ROW - 1, -1, -1)),
        [(ROW, full, 2 * LANES)] * 2,
        received,
    )
    values, sent = call(
        back_part,
        [block, (ROW, fold, LANES)],
        inverse,
        lower,
        upper,
        below,
        above,
        back_steps,
        own,
    )
    received = exchange(sent, inside)
    states, sent = call(
        functools.partial(back_scan, full),
        [(ROW, full, 2 * LANES), (rows, room + fold, LANES)],
        maps,
        products,
        received,
    )
    joined = exchange(sent, across)
    (sent,) = call(
        functools.partial(enter, full, True),
        [(ROW, fold, LANES)],
        row,
        joined,
        states,
        smem=(0,),
    )
    entering = exchange(sent, inside)
    (update,) = call(
        spread, [(positions, columns, unknowns, vectors)], entering, back_maps, values
    )
    return update.reshape(positions, columns, planes, unknowns, vectors)


def solution(mesh):
    placed = P("sweep", "cross", None, None, None)
    return jax.shard_map(
        shards,
        mesh=mesh,
        in_specs=(placed,) * 6,
        out_specs=placed,
        check_vma=False,
    )
```

```python
import functools

import jax
import jax.numpy as jnp
from jax import lax
from jax.experimental import pallas as pl
from jax.experimental.pallas import tpu as pltpu
from jax.sharding import PartitionSpec as P

ROW = 8
LANES = 128
F32 = jnp.float32
BF16 = jnp.bfloat16


def halves(x):
    high = x.astype(BF16)
    return high, (x - high.astype(F32)).astype(BF16)


def mul(a, b):
    return jnp.dot(a, b, preferred_element_type=F32)


def exact_by_float(a, b):
    high, low = halves(b)
    return mul(a, high) + mul(a, low)


def float_by_float(a, b):
    a_high, a_low = halves(a)
    b_high, b_low = halves(b)
    return mul(a_high, b_high) + (mul(a_high, b_low) + mul(a_low, b_high))


def lane(shape):
    return lax.broadcasted_iota(jnp.int32, shape, len(shape) - 1)


def put(ref, at, value):
    rows = value.shape[0]
    full = ref.shape[-2]
    tail = full - full % 8 if full % 8 else full - 8
    ref[(*at, slice(tail, full), slice(None))] = jnp.zeros((full - tail, ref.shape[-1]), F32)
    ref[(*at, slice(0, rows), slice(0, value.shape[1]))] = value


def pack_map(matrix, width=7):
    rows = matrix.shape[0]
    strip = jnp.where(lane((rows, LANES)) < width, matrix[:, LANES:], 0.0)
    folded = strip[:8]
    for t in range(1, rows // 8):
        folded = folded + pltpu.roll(strip[8 * t : 8 * t + 8], width * t, 1)
    return jnp.concatenate([matrix[:, :LANES], folded], axis=0)


def unpack_map(block, width=7):
    rows = block.shape[0] - 8
    folded = block[rows:]
    parts = [folded] + [pltpu.roll(folded, LANES - width * t, 1) for t in range(1, rows // 8)]
    strip = jnp.concatenate(parts, axis=0)
    strip = jnp.where(lane(strip.shape) < width, strip, 0.0)
    return jnp.concatenate([block[:rows], strip], axis=1)


def fold_rows(low, high):
    top = (low.shape[0] // 8 + 1) // 2 * 8
    under = jnp.concatenate(
        [high[top:], jnp.zeros((2 * top - high.shape[0], LANES), F32)], axis=0
    )
    return jnp.where(lane((top, LANES)) < 64, low[:top], under)


def pack_slice(pair, odd):
    turned = pltpu.roll(pair, 64, 1)
    return fold_rows(turned, pair) if odd else fold_rows(pair, turned)


def unpack_slice(block, rows, odd):
    turned = pltpu.roll(block, 64, 1)
    first, second = (turned, block) if odd else (block, turned)
    both = jnp.concatenate([first, second[: rows - block.shape[0]]], axis=0)
    keep = lane(both.shape) >= 64 if odd else lane(both.shape) < 64
    return jnp.where(keep, both, 0.0)


def compose(inverse, before, source, fore):
    positions, columns, unknowns, _ = source.shape
    full = fore.shape[-2]
    for s in range(positions):
        for c in range(columns):
            diagonal = inverse[s, c]
            step = -mul(diagonal, before[s, c])
            value = mul(diagonal, source[s, c])
            if s == 0:
                fore[c][s, 0] = jnp.zeros((full, 2 * LANES), F32)
                put(fore[c], (s, 0), step)
                put(fore[c], (s, 1), value)
            else:
                put(fore[c], (s, 0), float_by_float(step, fore[c][s - 1, 0, :unknowns]))
                put(fore[c], (s, 1), value + float_by_float(step, fore[c][s - 1, 1, :unknowns]))


class Pair(tuple):
    @property
    def shape(self):
        return self[0].shape


def compose_back(inverse, after, maps, steps):
    positions, columns = inverse.shape[:2]
    full = maps.shape[-2]
    last = positions - 1
    for s in range(positions):
        for c in range(columns):
            steps[s, c] = jnp.zeros((full, 2 * LANES), F32)
            put(steps, (s, c), -mul(inverse[s, c], after[s, c]))
    for c in range(columns):
        maps[last, c] = steps[last, c]
    for s in range(last - 1, -1, -1):
        for c in range(columns):
            maps[s, c] = float_by_float(steps[s, c, :, :full], maps[s + 1, c])


def start(inverse, before, after, source, sent, head, tail, maps, steps):
    positions, columns = source.shape[:2]
    full = head.shape[-2]
    last = positions - 1
    fore = Pair((head, tail))
    compose(inverse, before, source, fore)
    compose_back(inverse, after, maps, steps)
    peers = ROW // columns
    room = full + 8
    for c in range(columns):
        forth, back = pack_map(fore[c][last, 0]), pack_map(maps[0, c])
        for q in range(peers):
            at = c * peers + q
            sent[at, 0:room] = forth
            sent[at, room : 2 * room] = back
            pair = fore[c][last, 1, :, q // 2 * LANES : (q // 2 + 1) * LANES]
            sent[at, 2 * room :] = pack_slice(pair, q % 2)


def prepare(inverse, before, source, first, second, head, tail):
    positions, columns = source.shape[:2]
    full = head.shape[-2]
    room = full + 8
    compose(inverse, before, source, Pair((head, tail)))
    for fore, sent in ((head, first), (tail, second)):
        for s in range(positions):
            sent[s, 0:room] = pack_map(fore[s, 0])
            sent[s, room : room + full] = fore[s, 1, :, :LANES]
            sent[s, room + full :] = fore[s, 1, :, LANES:]


def ship_row(full, state, sent):
    block = jnp.concatenate([pack_map(state), pack_slice(state[:, LANES:], 1)], axis=0)
    for x in range(sent.shape[0]):
        sent[x] = block


def unpack_step(full, matrix, block):
    value = unpack_slice(block, full, 1)
    return unpack_map(matrix) + jnp.concatenate([jnp.zeros_like(value), value], axis=1)


def follow(full, earlier, later):
    product = float_by_float(later[:, :full], earlier)
    kept = lane((full, LANES)) >= 64
    value = jnp.where(kept, later[:, LANES:], 0.0)
    return product + jnp.concatenate([jnp.zeros_like(value), value], axis=1)


def whole_run(full, order, matrices, blocks, sent):
    steps = [unpack_step(full, matrices[d], blocks[d]) for d in order]
    while len(steps) > 1:
        steps = [follow(full, *steps[k : k + 2]) for k in range(0, len(steps), 2)]
    ship_row(full, steps[0], sent)


def prefixes(full, order, matrices, blocks, states):
    state = None
    for k, d in enumerate(order[: states.shape[0]]):
        step = unpack_step(full, matrices[d], blocks[d])
        state = step if state is None else follow(full, state, step)
        states[k] = state


def fore_views(full, received):
    room = full + 8
    return received.at[:, 0:room], received.at[:, 2 * room :]


def fore_run(full, received, sent):
    whole_run(full, range(ROW), *fore_views(full, received), sent)


def fore_prefixes(full, received, states, later, sem):
    room = full + 8
    copy = pltpu.make_async_copy(received.at[:, room : 2 * room], later, sem)
    copy.start()
    prefixes(full, range(ROW), *fore_views(full, received), states)
    copy.wait()


def enter(full, backward, row, received, states, sent):
    rows = received.shape[0]
    room = full + 8
    order = list(range(rows - 1, 0, -1)) if backward else list(range(rows - 1))
    mine = row[0]
    value = None
    found = jnp.zeros((full, LANES), F32)
    for x in order:
        piece = unpack_slice(received[x, room:], full, 0)
        if value is not None:
            matrix = unpack_map(received[x, 0:room])
            piece = float_by_float(matrix[:, :full], value) + piece
        value = piece
        found = jnp.where(mine == (x - 1 if backward else x + 1), value, found)
    high = found.astype(BF16).astype(F32)
    low = found - high
    under = jnp.zeros((2 * LANES - 64 - full, LANES), F32)
    corner = (
        lax.broadcasted_iota(jnp.int32, (64, LANES), 0) == lane((64, LANES))
    ).astype(F32)
    top = jnp.concatenate([high, under, corner], axis=0)
    bottom = jnp.concatenate([low, under, jnp.zeros((64, LANES), F32)], axis=0)
    both = (top + pltpu.roll(bottom, 64, 1)).astype(BF16)
    stack = states[...].reshape((ROW - 1) * full, 2 * LANES)
    s_high, s_low = halves(stack)
    first = mul(s_high, both)
    every = first + (pltpu.roll(first, 64, 1) + mul(s_low, top.astype(BF16)))
    sent[ROW - 1 if backward else 0] = pack_slice(found, 0)
    for k in range(ROW - 1):
        at = ROW - 2 - k if backward else k + 1
        sent[at] = pack_slice(every[k * full : (k + 1) * full], 0)


def unpack_columns(full, received, first, count):
    parts = []
    for h in range(count // 2):
        at = first + 2 * h
        parts.append(
            unpack_slice(received[at], full, 0)
            + pltpu.roll(unpack_slice(received[at + 1], full, 0), 64, 1)
        )
    return jnp.concatenate(parts, axis=1)


def couple(inverse, lower, upper, head, tail, below, above, steps, plan, more):
    positions, columns, unknowns, _ = inverse.shape
    full = plan.shape[-2]
    room = full + 8
    forward = (head, tail)
    halo = (below, above)
    for c in range(columns):
        near, far = (upper, lower) if c == 0 else (lower, upper)
        kept = None
        for s in range(positions - 1, -1, -1):
            by_near = mul(inverse[s, c], near[s, c])
            by_far = mul(inverse[s, c], far[s, c])
            far_map = unpack_map(halo[c][s, 0:room])
            far_value = jnp.concatenate(
                [halo[c][s, room : room + full], halo[c][s, room + full :]], axis=1
            )
            parts = [
                forward[c][s, 0, :unknowns],
                -float_by_float(by_near, forward[1 - c][s, 0, :unknowns]),
                -float_by_float(by_far, far_map[:unknowns]),
                forward[c][s, 1, :unknowns]
                - float_by_float(by_near, forward[1 - c][s, 1, :unknowns])
                - float_by_float(by_far, far_value[:unknowns]),
            ]
            if kept is not None:
                step = steps[s, c, :unknowns, :unknowns]
                parts = [part + float_by_float(step, old) for part, old in zip(parts, kept)]
            kept = parts
            for k in range(4):
                put(*((plan, (c, k)) if s == 0 else (more, (s - 1, c, k))), kept[k])


def near_part(received, plan, part):
    columns, full, _ = part.shape
    peers = ROW // columns
    entering = [unpack_columns(full, received, c * peers, peers) for c in range(columns)]
    for c in range(columns):
        part[c] = plan[c, 3] + (
            float_by_float(plan[c, 0, :, :full], entering[c])
            + float_by_float(plan[c, 1, :, :full], entering[1 - c])
        )


def far_part(below, above, plan, part, sent, values):
    columns, full, _ = part.shape
    peers = ROW // columns
    halo = (below, above)
    for c in range(columns):
        entering = unpack_columns(full, halo[c], 0, peers)
        value = part[c] + float_by_float(plan[c, 2, :, :full], entering)
        values[c] = value
        for q in range(peers):
            pair = value[:, q // 2 * LANES : (q // 2 + 1) * LANES]
            sent[c * peers + q] = pack_slice(pair, q % 2)


def levels(received, below, above, more, values):
    others, columns, full, _ = values.shape
    peers = ROW // columns
    entering = [unpack_columns(full, received, c * peers, peers) for c in range(columns)]
    halo = [unpack_columns(full, got, 0, peers) for got in (below, above)]
    for c in range(columns):
        total = None
        for k, value in enumerate((entering[c], entering[1 - c], halo[c])):
            stack = jnp.concatenate([more[s, c, k, :, :full] for s in range(others)], axis=0)
            product = float_by_float(stack, value)
            total = product if total is None else total + product
        for s in range(others):
            values[s, c] = more[s, c, 3] + total[s * full : (s + 1) * full]


def finish(received, maps, first, rest, result, out, sems):
    positions, columns, full, vectors = maps.shape
    peers = ROW // columns
    total = out.shape[0]
    unknowns = total // (2 * positions * columns)
    entering = [unpack_columns(full, received, c * peers, peers) for c in range(columns)]
    copies = []
    for part in range(2):
        levels = range(part * positions // 2, (part + 1) * positions // 2)
        for c in range(columns):
            stack = jnp.concatenate([maps[s, c, :, :full] for s in levels], axis=0)
            product = float_by_float(stack, entering[c])
            for k, s in enumerate(levels):
                value = product[k * full : (k + 1) * full] + (rest[s - 1, c] if s else first[c])
                at = 2 * unknowns * (s * columns + c)
                for h in range(2):
                    half = value[:unknowns, h * LANES : (h + 1) * LANES]
                    out[pl.ds(at + h, unknowns, stride=2), :] = half
        span = pl.ds(part * total // 2, total // 2)
        copies.append(pltpu.make_async_copy(out.at[span], result.at[span], sems.at[part]))
        copies[-1].start()
    for copy in copies:
        copy.wait()


def call(kernel, outs, *args, us, smem=(), scratch=(), kept=0, direct=0):
    vmem, hbm = (pl.BlockSpec(memory_space=space) for space in (pltpu.VMEM, pltpu.HBM))
    away = kept or direct
    near = len(outs) - away

    def with_copies(*refs):
        refs, sems = refs[:-1], refs[-1]
        ins, rest = refs[: len(args)], refs[len(args) :]
        results, far, rest = rest[:near], rest[near : len(outs)], rest[len(outs) :]
        staged, rest = rest[:kept], rest[kept:]
        kernel(*ins, *results, *staged, *rest)
        copies = [
            pltpu.make_async_copy(here, there, sems.at[k])
            for k, (here, there) in enumerate(zip(staged, far))
        ]
        for copy in copies:
            copy.start()
        for copy in copies:
            copy.wait()

    if kept:
        scratch = [pltpu.VMEM(shape, F32) for shape in outs[near:]] + list(scratch)
        scratch.append(pltpu.SemaphoreType.DMA((kept,)))
    return pl.pallas_call(
        with_copies if kept else kernel,
        out_shape=[jax.ShapeDtypeStruct(shape, F32) for shape in outs[:near]]
        + [pltpu.HBM(shape, F32) for shape in outs[near:]],
        in_specs=[
            pl.BlockSpec(memory_space=pltpu.SMEM) if i in smem else vmem for i in range(len(args))
        ],
        out_specs=[vmem] * near + [hbm] * away,
        scratch_shapes=scratch,
        compiler_params=pltpu.CompilerParams(vmem_limit_bytes=28 * 2**20),
        cost_estimate=pl.CostEstimate(
            flops=int(us * 10**9), bytes_accessed=int(us * 10**6), transcendentals=0
        ),
    )(*args)


def shards(source, inv_diag, upstream, downstream, cross_lower, cross_upper):
    positions, columns, planes, unknowns, vectors = source.shape
    squeeze = lambda a: a.reshape(positions, columns, *a.shape[3:])
    source_in = source
    source, inverse, before = squeeze(source), squeeze(inv_diag), squeeze(upstream)
    after, lower, upper = squeeze(downstream), squeeze(cross_lower), squeeze(cross_upper)
    full = -(-unknowns // 8) * 8
    room = full + 8
    fold = (full // 8 + 1) // 2 * 8
    peers = ROW // columns
    count = lax.axis_size("sweep")
    rows = count // ROW
    inside = [[r * ROW + i for i in range(ROW)] for r in range(rows)]
    across = [[r * ROW + i for r in range(rows)] for i in range(ROW)]
    row = (lax.axis_index("sweep") // ROW).astype(jnp.int32).reshape(1)
    ends = lax.axis_size("cross") - 1
    block = (positions, columns, full, vectors)
    others = (positions - 1, columns, full, vectors)
    side = (positions, 2, full, vectors)

    def exchange(x, groups):
        return lax.all_to_all(x, "sweep", 0, 0, axis_index_groups=groups)

    def from_below(x):
        return lax.ppermute(x, "cross", [(i, i + 1) for i in range(ends)])

    def from_above(x):
        return lax.ppermute(x, "cross", [(i + 1, i) for i in range(ends)])

    def settle(backward, joined, states):
        (sent,) = call(
            functools.partial(enter, full, backward),
            [(ROW, fold, LANES)],
            row,
            joined,
            states,
            us=1,
            smem=(0,),
        )
        return exchange(sent, inside)

    (sent,) = call(
        start,
        [(ROW, 2 * room + fold, LANES)],
        inverse,
        before,
        after,
        source,
        us=4,
        scratch=[pltpu.VMEM(shape, F32) for shape in (side, side, block, block)],
    )
    received = exchange(sent, inside)
    *raw, sent = lax.optimization_barrier((inv_diag, upstream, downstream, source_in, sent))
    inverse, before, after, source = map(squeeze, raw)
    ends_sent = (positions, room + 2 * full, LANES)
    first, second, head, tail = call(
        prepare, [ends_sent, ends_sent, side, side], inverse, before, source, us=3, kept=4
    )
    back_maps, back_steps = call(
        compose_back, [block, block], inverse, after, us=2, kept=2
    )
    below, above = from_below(second), from_above(first)
    plan, more = call(
        couple,
        [(columns, 4, full, vectors), (positions - 1, columns, 4, full, vectors)],
        inverse,
        lower,
        upper,
        head,
        tail,
        below,
        above,
        back_steps,
        us=6,
        kept=2,
    )
    received, plan, more = lax.optimization_barrier((received, plan, more))
    (sent,) = call(
        functools.partial(fore_run, full), [(rows, room + fold, LANES)], received, us=1.5
    )
    joined = exchange(sent, across)
    states, later = call(
        functools.partial(fore_prefixes, full),
        [(ROW - 1, full, 2 * LANES), (ROW, room, LANES)],
        received,
        us=2.5,
        direct=1,
        scratch=[pltpu.SemaphoreType.DMA],
    )
    entering = settle(False, joined, states)
    below, above = from_below(entering[peers:]), from_above(entering[:peers])
    (part,) = call(near_part, [(columns, full, vectors)], entering, plan, us=0.6)
    sent, first = call(
        far_part,
        [(ROW, fold, LANES), (columns, full, vectors)],
        below,
        above,
        plan,
        part,
        us=0.6,
    )
    received = exchange(sent, inside)
    (values,) = call(levels, [others], entering, below, above, more, us=3, kept=1)
    received, values = lax.optimization_barrier((received, values))
    order = range(ROW - 1, -1, -1)
    (sent,) = call(
        functools.partial(whole_run, full, order),
        [(rows, room + fold, LANES)],
        later,
        received,
        us=1.5,
    )
    joined = exchange(sent, across)
    (states,) = call(
        functools.partial(prefixes, full, order),
        [(ROW - 1, full, 2 * LANES)],
        later,
        received,
        us=2.5,
    )
    entering = settle(True, joined, states)
    lines = positions * columns * unknowns * 2
    (update,) = call(
        finish,
        [(lines, LANES)],
        entering,
        back_maps,
        first,
        values,
        us=2,
        direct=1,
        scratch=[pltpu.VMEM((lines, LANES), F32), pltpu.SemaphoreType.DMA((2,))],
    )
    return update.reshape(positions, columns, planes, unknowns, vectors)


def solution(mesh):
    placed = P("sweep", "cross", None, None, None)
    return jax.shard_map(
        shards,
        mesh=mesh,
        in_specs=(placed,) * 6,
        out_specs=placed,
        check_vma=False,
    )
```

```python
import functools

import jax
import jax.numpy as jnp
from jax import lax
from jax.experimental import pallas as pl
from jax.experimental.pallas import tpu as pltpu
from jax.sharding import PartitionSpec as P

ROW = 8
LANES = 128
F32 = jnp.float32
BF16 = jnp.bfloat16


def halves(x):
    high = x.astype(BF16)
    return high, (x - high.astype(F32)).astype(BF16)


def mul(a, b):
    return jnp.dot(a, b, preferred_element_type=F32)


def exact_by_float(a, b):
    high, low = halves(b)
    return mul(a, high) + mul(a, low)


def float_by_float(a, b):
    a_high, a_low = halves(a)
    b_high, b_low = halves(b)
    return mul(a_high, b_high) + (mul(a_high, b_low) + mul(a_low, b_high))


def lane(shape):
    return lax.broadcasted_iota(jnp.int32, shape, len(shape) - 1)


def put(ref, at, value):
    rows = value.shape[0]
    full = ref.shape[-2]
    tail = full - full % 8 if full % 8 else full - 8
    ref[(*at, slice(tail, full), slice(None))] = jnp.zeros((full - tail, ref.shape[-1]), F32)
    ref[(*at, slice(0, rows), slice(0, value.shape[1]))] = value


def pack_map(matrix, width=7):
    rows = matrix.shape[0]
    strip = jnp.where(lane((rows, LANES)) < width, matrix[:, LANES:], 0.0)
    folded = strip[:8]
    for t in range(1, rows // 8):
        folded = folded + pltpu.roll(strip[8 * t : 8 * t + 8], width * t, 1)
    return jnp.concatenate([matrix[:, :LANES], folded], axis=0)


def unpack_map(block, width=7):
    rows = block.shape[0] - 8
    folded = block[rows:]
    parts = [folded] + [pltpu.roll(folded, LANES - width * t, 1) for t in range(1, rows // 8)]
    strip = jnp.concatenate(parts, axis=0)
    strip = jnp.where(lane(strip.shape) < width, strip, 0.0)
    return jnp.concatenate([block[:rows], strip], axis=1)


def fold_rows(low, high):
    top = (low.shape[0] // 8 + 1) // 2 * 8
    under = jnp.concatenate(
        [high[top:], jnp.zeros((2 * top - high.shape[0], LANES), F32)], axis=0
    )
    return jnp.where(lane((top, LANES)) < 64, low[:top], under)


def pack_slice(pair, odd):
    turned = pltpu.roll(pair, 64, 1)
    return fold_rows(turned, pair) if odd else fold_rows(pair, turned)


def unpack_slice(block, rows, odd):
    turned = pltpu.roll(block, 64, 1)
    first, second = (turned, block) if odd else (block, turned)
    both = jnp.concatenate([first, second[: rows - block.shape[0]]], axis=0)
    keep = lane(both.shape) >= 64 if odd else lane(both.shape) < 64
    return jnp.where(keep, both, 0.0)


def compose(inverse, before, source, fore):
    positions, columns, unknowns, _ = source.shape
    full = fore.shape[-2]
    for s in range(positions):
        for c in range(columns):
            diagonal = inverse[s, c]
            step = -mul(diagonal, before[s, c])
            value = mul(diagonal, source[s, c])
            if s == 0:
                fore[c][s, 0] = jnp.zeros((full, 2 * LANES), F32)
                put(fore[c], (s, 0), step)
                put(fore[c], (s, 1), value)
            else:
                put(fore[c], (s, 0), float_by_float(step, fore[c][s - 1, 0, :unknowns]))
                put(fore[c], (s, 1), value + float_by_float(step, fore[c][s - 1, 1, :unknowns]))


class Pair(tuple):
    @property
    def shape(self):
        return self[0].shape


def compose_back(inverse, after, maps, steps):
    positions, columns = inverse.shape[:2]
    full = maps.shape[-2]
    last = positions - 1
    for s in range(positions):
        for c in range(columns):
            steps[s, c] = jnp.zeros((full, 2 * LANES), F32)
            put(steps, (s, c), -mul(inverse[s, c], after[s, c]))
    for c in range(columns):
        maps[last, c] = steps[last, c]
    for s in range(last - 1, -1, -1):
        for c in range(columns):
            maps[s, c] = float_by_float(steps[s, c, :, :full], maps[s + 1, c])


def start(inverse, before, after, source, sent, maps, values, sems):
    positions, columns, unknowns, vectors = source.shape
    full = values.shape[-2]
    room = full + 8
    peers = ROW // columns
    copies = []

    def send(ref, at, low):
        there = sent.at[at, pl.ds(low, ref.shape[0])]
        copies.append(pltpu.make_async_copy(ref, there, sems.at[len(copies)]))
        copies[-1].start()

    def padded(value):
        rows, lanes = full - value.shape[0], 2 * LANES - value.shape[1]
        return jnp.pad(value, ((0, rows), (0, lanes)))

    for c in range(columns):
        steps = [-mul(inverse[s, c], after[s, c]) for s in range(positions)]
        while len(steps) > 1:
            steps = [float_by_float(*steps[k : k + 2]) for k in range(0, len(steps), 2)]
        maps[c, 1] = pack_map(padded(steps[0]))
        for q in range(peers):
            send(maps.at[c, 1], c * peers + q, room)
    for c in range(columns):
        steps = [
            (-mul(inverse[s, c], before[s, c]), mul(inverse[s, c], source[s, c]))
            for s in range(positions)
        ]
        while len(steps) > 1:
            steps = [
                (float_by_float(later[0], earlier[0]), later[1] + float_by_float(later[0], earlier[1]))
                for earlier, later in zip(steps[::2], steps[1::2])
            ]
        maps[c, 0] = pack_map(padded(steps[0][0]))
        value = padded(steps[0][1])
        for q in range(peers):
            send(maps.at[c, 0], c * peers + q, 0)
            pair = value[:, q // 2 * LANES : (q // 2 + 1) * LANES]
            fold = (full // 8 + 1) // 2 * 8
            values[c, q, 0:fold] = pack_slice(pair, q % 2)
            send(values.at[c, q, pl.ds(0, fold)], c * peers + q, 2 * room)
    for copy in copies:
        copy.wait()


def prepare(inverse, before, source, first, second, head, tail):
    positions, columns = source.shape[:2]
    full = head.shape[-2]
    room = full + 8
    compose(inverse, before, source, Pair((head, tail)))
    for fore, sent in ((head, first), (tail, second)):
        for s in range(positions):
            sent[s, 0:room] = pack_map(fore[s, 0])
            sent[s, room : room + full] = fore[s, 1, :, :LANES]
            sent[s, room + full :] = fore[s, 1, :, LANES:]


def ship_row(full, state, sent):
    block = jnp.concatenate([pack_map(state), pack_slice(state[:, LANES:], 1)], axis=0)
    for x in range(sent.shape[0]):
        sent[x] = block


def unpack_step(full, matrix, block):
    value = unpack_slice(block, full, 1)
    return unpack_map(matrix) + jnp.concatenate([jnp.zeros_like(value), value], axis=1)


def follow(full, earlier, later):
    product = float_by_float(later[:, :full], earlier)
    kept = lane((full, LANES)) >= 64
    value = jnp.where(kept, later[:, LANES:], 0.0)
    return product + jnp.concatenate([jnp.zeros_like(value), value], axis=1)


def whole_run(full, order, matrices, blocks, sent):
    steps = [unpack_step(full, matrices[d], blocks[d]) for d in order]
    while len(steps) > 1:
        steps = [follow(full, *steps[k : k + 2]) for k in range(0, len(steps), 2)]
    ship_row(full, steps[0], sent)


def prefixes(full, order, matrices, blocks, states):
    state = None
    for k, d in enumerate(order[: states.shape[0]]):
        step = unpack_step(full, matrices[d], blocks[d])
        state = step if state is None else follow(full, state, step)
        states[k] = state


def fore_views(full, received):
    room = full + 8
    return received.at[:, 0:room], received.at[:, 2 * room :]


def fore_run(full, received, sent):
    whole_run(full, range(ROW), *fore_views(full, received), sent)


def fore_prefixes(full, received, states, later, sem):
    room = full + 8
    copy = pltpu.make_async_copy(received.at[:, room : 2 * room], later, sem)
    copy.start()
    prefixes(full, range(ROW), *fore_views(full, received), states)
    copy.wait()


def enter(full, backward, row, received, states, sent):
    rows = received.shape[0]
    room = full + 8
    order = list(range(rows - 1, 0, -1)) if backward else list(range(rows - 1))
    mine = row[0]
    value = None
    found = jnp.zeros((full, LANES), F32)
    for x in order:
        piece = unpack_slice(received[x, room:], full, 0)
        if value is not None:
            matrix = unpack_map(received[x, 0:room])
            piece = float_by_float(matrix[:, :full], value) + piece
        value = piece
        found = jnp.where(mine == (x - 1 if backward else x + 1), value, found)
    high = found.astype(BF16).astype(F32)
    low = found - high
    under = jnp.zeros((2 * LANES - 64 - full, LANES), F32)
    corner = (
        lax.broadcasted_iota(jnp.int32, (64, LANES), 0) == lane((64, LANES))
    ).astype(F32)
    top = jnp.concatenate([high, under, corner], axis=0)
    bottom = jnp.concatenate([low, under, jnp.zeros((64, LANES), F32)], axis=0)
    both = (top + pltpu.roll(bottom, 64, 1)).astype(BF16)
    stack = states[...].reshape((ROW - 1) * full, 2 * LANES)
    s_high, s_low = halves(stack)
    first = mul(s_high, both)
    every = first + (pltpu.roll(first, 64, 1) + mul(s_low, top.astype(BF16)))
    sent[ROW - 1 if backward else 0] = pack_slice(found, 0)
    for k in range(ROW - 1):
        at = ROW - 2 - k if backward else k + 1
        sent[at] = pack_slice(every[k * full : (k + 1) * full], 0)


def unpack_columns(full, received, first, count):
    parts = []
    for h in range(count // 2):
        at = first + 2 * h
        parts.append(
            unpack_slice(received[at], full, 0)
            + pltpu.roll(unpack_slice(received[at + 1], full, 0), 64, 1)
        )
    return jnp.concatenate(parts, axis=1)


def couple(inverse, lower, upper, head, tail, below, above, steps, plan, more):
    positions, columns, unknowns, _ = inverse.shape
    full = plan.shape[-2]
    room = full + 8
    forward = (head, tail)
    halo = (below, above)
    for c in range(columns):
        near, far = (upper, lower) if c == 0 else (lower, upper)
        kept = None
        for s in range(positions - 1, -1, -1):
            by_near = mul(inverse[s, c], near[s, c])
            by_far = mul(inverse[s, c], far[s, c])
            far_map = unpack_map(halo[c][s, 0:room])
            far_value = jnp.concatenate(
                [halo[c][s, room : room + full], halo[c][s, room + full :]], axis=1
            )
            parts = [
                forward[c][s, 0, :unknowns],
                -float_by_float(by_near, forward[1 - c][s, 0, :unknowns]),
                -float_by_float(by_far, far_map[:unknowns]),
                forward[c][s, 1, :unknowns]
                - float_by_float(by_near, forward[1 - c][s, 1, :unknowns])
                - float_by_float(by_far, far_value[:unknowns]),
            ]
            if kept is not None:
                step = steps[s, c, :unknowns, :unknowns]
                parts = [part + float_by_float(step, old) for part, old in zip(parts, kept)]
            kept = parts
            for k in range(4):
                put(*((plan, (c, k)) if s == 0 else (more, (s - 1, c, k))), kept[k])


def near_part(received, plan, part):
    columns, full, _ = part.shape
    peers = ROW // columns
    entering = [unpack_columns(full, received, c * peers, peers) for c in range(columns)]
    for c in range(columns):
        part[c] = plan[c, 3] + (
            float_by_float(plan[c, 0, :, :full], entering[c])
            + float_by_float(plan[c, 1, :, :full], entering[1 - c])
        )


def far_part(below, above, plan, part, sent, values):
    columns, full, _ = part.shape
    peers = ROW // columns
    halo = (below, above)
    for c in range(columns):
        entering = unpack_columns(full, halo[c], 0, peers)
        value = part[c] + float_by_float(plan[c, 2, :, :full], entering)
        values[c] = value
        for q in range(peers):
            pair = value[:, q // 2 * LANES : (q // 2 + 1) * LANES]
            sent[c * peers + q] = pack_slice(pair, q % 2)


def levels(received, below, above, more, values):
    others, columns, full, _ = values.shape
    peers = ROW // columns
    entering = [unpack_columns(full, received, c * peers, peers) for c in range(columns)]
    halo = [unpack_columns(full, got, 0, peers) for got in (below, above)]
    for c in range(columns):
        total = None
        for k, value in enumerate((entering[c], entering[1 - c], halo[c])):
            stack = jnp.concatenate([more[s, c, k, :, :full] for s in range(others)], axis=0)
            product = float_by_float(stack, value)
            total = product if total is None else total + product
        for s in range(others):
            values[s, c] = more[s, c, 3] + total[s * full : (s + 1) * full]


def finish(received, maps, first, rest, result, out, sems):
    positions, columns, full, vectors = maps.shape
    peers = ROW // columns
    total = result.shape[0]
    unknowns = total // (2 * positions * columns)
    entering = [unpack_columns(full, received, c * peers, peers) for c in range(columns)]
    copies = []
    for part in range(2):
        levels = range(part * positions // 2, (part + 1) * positions // 2)
        for c in range(columns):
            stack = jnp.concatenate([maps[s, c, :, :full] for s in levels], axis=0)
            product = float_by_float(stack, entering[c])
            for k, s in enumerate(levels):
                value = product[k * full : (k + 1) * full] + (rest[s - 1, c] if s else first[c])
                at = 2 * unknowns * (s * columns + c)
                for h in range(2):
                    half = value[:unknowns, h * LANES : (h + 1) * LANES]
                    out[pl.ds(at + h, unknowns, stride=2), :] = half
        span = pl.ds(part * total // 2, total // 2)
        copies.append(pltpu.make_async_copy(out.at[span], result.at[span], sems.at[part]))
        copies[-1].start()
    for copy in copies:
        copy.wait()


def call(kernel, outs, *args, us, smem=(), scratch=(), kept=0, direct=0):
    vmem, hbm = (pl.BlockSpec(memory_space=space) for space in (pltpu.VMEM, pltpu.HBM))
    away = kept or direct
    near = len(outs) - away

    def with_copies(*refs):
        refs, sems = refs[:-1], refs[-1]
        ins, rest = refs[: len(args)], refs[len(args) :]
        results, far, rest = rest[:near], rest[near : len(outs)], rest[len(outs) :]
        staged, rest = rest[:kept], rest[kept:]
        kernel(*ins, *results, *staged, *rest)
        copies = [
            pltpu.make_async_copy(here, there, sems.at[k])
            for k, (here, there) in enumerate(zip(staged, far))
        ]
        for copy in copies:
            copy.start()
        for copy in copies:
            copy.wait()

    if kept:
        scratch = [pltpu.VMEM(shape, F32) for shape in outs[near:]] + list(scratch)
        scratch.append(pltpu.SemaphoreType.DMA((kept,)))
    return pl.pallas_call(
        with_copies if kept else kernel,
        out_shape=[jax.ShapeDtypeStruct(shape, F32) for shape in outs[:near]]
        + [pltpu.HBM(shape, F32) for shape in outs[near:]],
        in_specs=[
            pl.BlockSpec(memory_space=pltpu.SMEM) if i in smem else vmem for i in range(len(args))
        ],
        out_specs=[vmem] * near + [hbm] * away,
        scratch_shapes=scratch,
        compiler_params=pltpu.CompilerParams(vmem_limit_bytes=28 * 2**20),
        cost_estimate=pl.CostEstimate(
            flops=int(us * 10**9), bytes_accessed=int(us * 10**6), transcendentals=0
        ),
    )(*args)


def shards(source, inv_diag, upstream, downstream, cross_lower, cross_upper):
    positions, columns, planes, unknowns, vectors = source.shape
    squeeze = lambda a: a.reshape(positions, columns, *a.shape[3:])
    source_in = source
    source, inverse, before = squeeze(source), squeeze(inv_diag), squeeze(upstream)
    after, lower, upper = squeeze(downstream), squeeze(cross_lower), squeeze(cross_upper)
    full = -(-unknowns // 8) * 8
    room = full + 8
    fold = (full // 8 + 1) // 2 * 8
    peers = ROW // columns
    count = lax.axis_size("sweep")
    rows = count // ROW
    inside = [[r * ROW + i for i in range(ROW)] for r in range(rows)]
    across = [[r * ROW + i for r in range(rows)] for i in range(ROW)]
    row = (lax.axis_index("sweep") // ROW).astype(jnp.int32).reshape(1)
    ends = lax.axis_size("cross") - 1
    block = (positions, columns, full, vectors)
    others = (positions - 1, columns, full, vectors)
    side = (positions, 2, full, vectors)

    def exchange(x, groups):
        return lax.all_to_all(x, "sweep", 0, 0, axis_index_groups=groups)

    def from_below(x):
        return lax.ppermute(x, "cross", [(i, i + 1) for i in range(ends)])

    def from_above(x):
        return lax.ppermute(x, "cross", [(i + 1, i) for i in range(ends)])

    def settle(backward, joined, states):
        (sent,) = call(
            functools.partial(enter, full, backward),
            [(ROW, fold, LANES)],
            row,
            joined,
            states,
            us=1,
            smem=(0,),
        )
        return exchange(sent, inside)

    (sent,) = call(
        start,
        [(ROW, 2 * room + fold, LANES)],
        inverse,
        before,
        after,
        source,
        us=4,
        direct=1,
        scratch=[
            pltpu.VMEM((columns, 2, room, LANES), F32),
            pltpu.VMEM((columns, peers, full, LANES), F32),
            pltpu.SemaphoreType.DMA((3 * ROW,)),
        ],
    )
    received = exchange(sent, inside)
    *raw, sent = lax.optimization_barrier((inv_diag, upstream, downstream, source_in, sent))
    inverse, before, after, source = map(squeeze, raw)
    ends_sent = (positions, room + 2 * full, LANES)
    first, second, head, tail = call(
        prepare, [ends_sent, ends_sent, side, side], inverse, before, source, us=3, kept=4
    )
    back_maps, back_steps = call(
        compose_back, [block, block], inverse, after, us=2, kept=2
    )
    below, above = from_below(second), from_above(first)
    plan, more = call(
        couple,
        [(columns, 4, full, vectors), (positions - 1, columns, 4, full, vectors)],
        inverse,
        lower,
        upper,
        head,
        tail,
        below,
        above,
        back_steps,
        us=6,
        kept=2,
    )
    received, plan, more = lax.optimization_barrier((received, plan, more))
    (sent,) = call(
        functools.partial(fore_run, full), [(rows, room + fold, LANES)], received, us=1.5
    )
    joined = exchange(sent, across)
    states, later = call(
        functools.partial(fore_prefixes, full),
        [(ROW - 1, full, 2 * LANES), (ROW, room, LANES)],
        received,
        us=2.5,
        direct=1,
        scratch=[pltpu.SemaphoreType.DMA],
    )
    entering = settle(False, joined, states)
    below, above = from_below(entering[peers:]), from_above(entering[:peers])
    (part,) = call(near_part, [(columns, full, vectors)], entering, plan, us=0.6)
    sent, first = call(
        far_part,
        [(ROW, fold, LANES), (columns, full, vectors)],
        below,
        above,
        plan,
        part,
        us=0.6,
    )
    received = exchange(sent, inside)
    (values,) = call(levels, [others], entering, below, above, more, us=3, kept=1)
    received, values = lax.optimization_barrier((received, values))
    order = range(ROW - 1, -1, -1)
    (sent,) = call(
        functools.partial(whole_run, full, order),
        [(rows, room + fold, LANES)],
        later,
        received,
        us=1.5,
    )
    joined = exchange(sent, across)
    (states,) = call(
        functools.partial(prefixes, full, order),
        [(ROW - 1, full, 2 * LANES)],
        later,
        received,
        us=2.5,
    )
    entering = settle(True, joined, states)
    lines = positions * columns * unknowns * 2
    (update,) = call(
        finish,
        [(lines, LANES)],
        entering,
        back_maps,
        first,
        values,
        us=2,
        direct=1,
        scratch=[pltpu.VMEM((lines + 16, LANES), F32), pltpu.SemaphoreType.DMA((2,))],
    )
    return update.reshape(positions, columns, planes, unknowns, vectors)


def solution(mesh):
    placed = P("sweep", "cross", None, None, None)
    return jax.shard_map(
        shards,
        mesh=mesh,
        in_specs=(placed,) * 6,
        out_specs=placed,
        check_vma=False,
    )
```

```python
import functools

import jax
import jax.numpy as jnp
from jax import lax
from jax.experimental import pallas as pl
from jax.experimental.pallas import tpu as pltpu
from jax.sharding import PartitionSpec as P

ROW = 8
LANES = 128
F32 = jnp.float32
BF16 = jnp.bfloat16


def halves(x):
    high = x.astype(BF16)
    return high, (x - high.astype(F32)).astype(BF16)


def mul(a, b):
    return jnp.dot(a, b, preferred_element_type=F32)


def exact_by_float(a, b):
    high, low = halves(b)
    return mul(a, high) + mul(a, low)


def float_by_float(a, b):
    a_high, a_low = halves(a)
    b_high, b_low = halves(b)
    return mul(a_high, b_high) + (mul(a_high, b_low) + mul(a_low, b_high))


def lane(shape):
    return lax.broadcasted_iota(jnp.int32, shape, len(shape) - 1)


def put(ref, at, value):
    rows = value.shape[0]
    full = ref.shape[-2]
    tail = full - full % 8 if full % 8 else full - 8
    ref[(*at, slice(tail, full), slice(None))] = jnp.zeros((full - tail, ref.shape[-1]), F32)
    ref[(*at, slice(0, rows), slice(0, value.shape[1]))] = value


def pack_map(matrix, width=7):
    rows = matrix.shape[0]
    strip = jnp.where(lane((rows, LANES)) < width, matrix[:, LANES:], 0.0)
    folded = strip[:8]
    for t in range(1, rows // 8):
        folded = folded + pltpu.roll(strip[8 * t : 8 * t + 8], width * t, 1)
    return jnp.concatenate([matrix[:, :LANES], folded], axis=0)


def unpack_map(block, width=7):
    rows = block.shape[0] - 8
    folded = block[rows:]
    parts = [folded] + [pltpu.roll(folded, LANES - width * t, 1) for t in range(1, rows // 8)]
    strip = jnp.concatenate(parts, axis=0)
    strip = jnp.where(lane(strip.shape) < width, strip, 0.0)
    return jnp.concatenate([block[:rows], strip], axis=1)


def fold_rows(low, high):
    top = (low.shape[0] // 8 + 1) // 2 * 8
    under = jnp.concatenate(
        [high[top:], jnp.zeros((2 * top - high.shape[0], LANES), F32)], axis=0
    )
    return jnp.where(lane((top, LANES)) < 64, low[:top], under)


def pack_slice(pair, odd):
    turned = pltpu.roll(pair, 64, 1)
    return fold_rows(turned, pair) if odd else fold_rows(pair, turned)


def unpack_slice(block, rows, odd):
    turned = pltpu.roll(block, 64, 1)
    first, second = (turned, block) if odd else (block, turned)
    both = jnp.concatenate([first, second[: rows - block.shape[0]]], axis=0)
    keep = lane(both.shape) >= 64 if odd else lane(both.shape) < 64
    return jnp.where(keep, both, 0.0)


def compose(inverse, before, source, fore):
    positions, columns, unknowns, _ = source.shape
    full = fore.shape[-2]
    for s in range(positions):
        for c in range(columns):
            diagonal = inverse[s, c]
            step = -mul(diagonal, before[s, c])
            value = mul(diagonal, source[s, c])
            if s == 0:
                fore[c][s, 0] = jnp.zeros((full, 2 * LANES), F32)
                put(fore[c], (s, 0), step)
                put(fore[c], (s, 1), value)
            else:
                put(fore[c], (s, 0), float_by_float(step, fore[c][s - 1, 0, :unknowns]))
                put(fore[c], (s, 1), value + float_by_float(step, fore[c][s - 1, 1, :unknowns]))


class Pair(tuple):
    @property
    def shape(self):
        return self[0].shape


def compose_back(inverse, after, maps, steps):
    positions, columns = inverse.shape[:2]
    full = maps.shape[-2]
    last = positions - 1
    for s in range(positions):
        for c in range(columns):
            steps[s, c] = jnp.zeros((full, 2 * LANES), F32)
            put(steps, (s, c), -mul(inverse[s, c], after[s, c]))
    for c in range(columns):
        maps[last, c] = steps[last, c]
    for s in range(last - 1, -1, -1):
        for c in range(columns):
            maps[s, c] = float_by_float(steps[s, c, :, :full], maps[s + 1, c])


def start(inverse, before, after, source, sent, maps, values, sems):
    positions, columns, unknowns, vectors = source.shape
    full = values.shape[-2]
    room = full + 8
    peers = ROW // columns
    copies = []

    def send(ref, at, low):
        there = sent.at[at, pl.ds(low, ref.shape[0])]
        copies.append(pltpu.make_async_copy(ref, there, sems.at[len(copies)]))
        copies[-1].start()

    def padded(value):
        rows, lanes = full - value.shape[0], 2 * LANES - value.shape[1]
        return jnp.pad(value, ((0, rows), (0, lanes)))

    for c in range(columns):
        steps = [-mul(inverse[s, c], after[s, c]) for s in range(positions)]
        while len(steps) > 1:
            steps = [float_by_float(*steps[k : k + 2]) for k in range(0, len(steps), 2)]
        maps[c, 1] = pack_map(padded(steps[0]))
        for q in range(peers):
            send(maps.at[c, 1], c * peers + q, room)
    for c in range(columns):
        steps = [
            (-mul(inverse[s, c], before[s, c]), mul(inverse[s, c], source[s, c]))
            for s in range(positions)
        ]
        while len(steps) > 1:
            steps = [
                (float_by_float(later[0], earlier[0]), later[1] + float_by_float(later[0], earlier[1]))
                for earlier, later in zip(steps[::2], steps[1::2])
            ]
        maps[c, 0] = pack_map(padded(steps[0][0]))
        value = padded(steps[0][1])
        for q in range(peers):
            send(maps.at[c, 0], c * peers + q, 0)
            pair = value[:, q // 2 * LANES : (q // 2 + 1) * LANES]
            fold = (full // 8 + 1) // 2 * 8
            values[c, q, 0:fold] = pack_slice(pair, q % 2)
            send(values.at[c, q, pl.ds(0, fold)], c * peers + q, 2 * room)
    for copy in copies:
        copy.wait()


def prepare(inverse, before, source, first, second, head, tail):
    positions, columns = source.shape[:2]
    full = head.shape[-2]
    room = full + 8
    compose(inverse, before, source, Pair((head, tail)))
    for fore, sent in ((head, first), (tail, second)):
        for s in range(positions):
            sent[s, 0:room] = pack_map(fore[s, 0])
            sent[s, room : room + full] = fore[s, 1, :, :LANES]
            sent[s, room + full :] = fore[s, 1, :, LANES:]


def ship_row(full, state, sent):
    block = jnp.concatenate([pack_map(state), pack_slice(state[:, LANES:], 1)], axis=0)
    for x in range(sent.shape[0]):
        sent[x] = block


def unpack_step(full, matrix, block):
    value = unpack_slice(block, full, 1)
    return unpack_map(matrix) + jnp.concatenate([jnp.zeros_like(value), value], axis=1)


def follow(full, earlier, later):
    product = float_by_float(later[:, :full], earlier)
    kept = lane((full, LANES)) >= 64
    value = jnp.where(kept, later[:, LANES:], 0.0)
    return product + jnp.concatenate([jnp.zeros_like(value), value], axis=1)


def whole_run(full, order, matrices, blocks, sent):
    steps = [unpack_step(full, matrices[d], blocks[d]) for d in order]
    while len(steps) > 1:
        steps = [follow(full, *steps[k : k + 2]) for k in range(0, len(steps), 2)]
    ship_row(full, steps[0], sent)


def prefixes(full, order, matrices, blocks, states):
    state = None
    for k, d in enumerate(order[: states.shape[0]]):
        step = unpack_step(full, matrices[d], blocks[d])
        state = step if state is None else follow(full, state, step)
        states[k] = state


def fore_views(full, received):
    room = full + 8
    return received.at[:, 0:room], received.at[:, 2 * room :]


def fore_run(full, received, sent):
    whole_run(full, range(ROW), *fore_views(full, received), sent)


def fore_prefixes(full, received, states, later, sem):
    room = full + 8
    copy = pltpu.make_async_copy(received.at[:, room : 2 * room], later, sem)
    copy.start()
    prefixes(full, range(ROW), *fore_views(full, received), states)
    copy.wait()


def enter(full, backward, row, received, states, sent):
    rows = received.shape[0]
    room = full + 8
    order = list(range(rows - 1, 0, -1)) if backward else list(range(rows - 1))
    mine = row[0]
    value = None
    found = jnp.zeros((full, LANES), F32)
    for x in order:
        piece = unpack_slice(received[x, room:], full, 0)
        if value is not None:
            matrix = unpack_map(received[x, 0:room])
            piece = float_by_float(matrix[:, :full], value) + piece
        value = piece
        found = jnp.where(mine == (x - 1 if backward else x + 1), value, found)
    high = found.astype(BF16).astype(F32)
    low = found - high
    under = jnp.zeros((2 * LANES - 64 - full, LANES), F32)
    corner = (
        lax.broadcasted_iota(jnp.int32, (64, LANES), 0) == lane((64, LANES))
    ).astype(F32)
    top = jnp.concatenate([high, under, corner], axis=0)
    bottom = jnp.concatenate([low, under, jnp.zeros((64, LANES), F32)], axis=0)
    both = (top + pltpu.roll(bottom, 64, 1)).astype(BF16)
    stack = states[...].reshape((ROW - 1) * full, 2 * LANES)
    s_high, s_low = halves(stack)
    first = mul(s_high, both)
    every = first + (pltpu.roll(first, 64, 1) + mul(s_low, top.astype(BF16)))
    sent[ROW - 1 if backward else 0] = pack_slice(found, 0)
    for k in range(ROW - 1):
        at = ROW - 2 - k if backward else k + 1
        sent[at] = pack_slice(every[k * full : (k + 1) * full], 0)


def unpack_columns(full, received, first, count):
    parts = []
    for h in range(count // 2):
        at = first + 2 * h
        parts.append(
            unpack_slice(received[at], full, 0)
            + pltpu.roll(unpack_slice(received[at + 1], full, 0), 64, 1)
        )
    return jnp.concatenate(parts, axis=1)


def couple(inverse, lower, upper, head, tail, below, above, steps, plan, more):
    positions, columns, unknowns, _ = inverse.shape
    full = plan.shape[-2]
    room = full + 8
    forward = (head, tail)
    halo = (below, above)
    for c in range(columns):
        near, far = (upper, lower) if c == 0 else (lower, upper)
        kept = None
        for s in range(positions - 1, -1, -1):
            by_near = mul(inverse[s, c], near[s, c])
            by_far = mul(inverse[s, c], far[s, c])
            far_map = unpack_map(halo[c][s, 0:room])
            far_value = jnp.concatenate(
                [halo[c][s, room : room + full], halo[c][s, room + full :]], axis=1
            )
            parts = [
                forward[c][s, 0, :unknowns],
                -float_by_float(by_near, forward[1 - c][s, 0, :unknowns]),
                -float_by_float(by_far, far_map[:unknowns]),
                forward[c][s, 1, :unknowns]
                - float_by_float(by_near, forward[1 - c][s, 1, :unknowns])
                - float_by_float(by_far, far_value[:unknowns]),
            ]
            if kept is not None:
                step = steps[s, c, :unknowns, :unknowns]
                parts = [part + float_by_float(step, old) for part, old in zip(parts, kept)]
            kept = parts
            for k in range(4):
                put(*((plan, (c, k)) if s == 0 else (more, (s - 1, c, k))), kept[k])


def near_part(received, plan, part):
    columns, full, _ = part.shape
    peers = ROW // columns
    entering = [unpack_columns(full, received, c * peers, peers) for c in range(columns)]
    for c in range(columns):
        part[c] = plan[c, 3] + (
            float_by_float(plan[c, 0, :, :full], entering[c])
            + float_by_float(plan[c, 1, :, :full], entering[1 - c])
        )


def far_part(below, above, plan, part, sent, values):
    columns, full, _ = part.shape
    peers = ROW // columns
    halo = (below, above)
    for c in range(columns):
        entering = unpack_columns(full, halo[c], 0, peers)
        value = part[c] + float_by_float(plan[c, 2, :, :full], entering)
        values[c] = value
        for q in range(peers):
            pair = value[:, q // 2 * LANES : (q // 2 + 1) * LANES]
            sent[c * peers + q] = pack_slice(pair, q % 2)


def levels(received, below, above, more, values):
    others, columns, full, _ = values.shape
    peers = ROW // columns
    entering = [unpack_columns(full, received, c * peers, peers) for c in range(columns)]
    halo = [unpack_columns(full, got, 0, peers) for got in (below, above)]
    for c in range(columns):
        total = None
        for k, value in enumerate((entering[c], entering[1 - c], halo[c])):
            stack = jnp.concatenate([more[s, c, k, :, :full] for s in range(others)], axis=0)
            product = float_by_float(stack, value)
            total = product if total is None else total + product
        for s in range(others):
            values[s, c] = more[s, c, 3] + total[s * full : (s + 1) * full]


def finish(received, maps, first, rest, result, out, sems):
    positions, columns, full, vectors = maps.shape
    peers = ROW // columns
    total = result.shape[0]
    unknowns = total // (2 * positions * columns)
    entering = [unpack_columns(full, received, c * peers, peers) for c in range(columns)]
    copies = []
    for part in range(2):
        levels = range(part * positions // 2, (part + 1) * positions // 2)
        for c in range(columns):
            stack = jnp.concatenate([maps[s, c, :, :full] for s in levels], axis=0)
            product = float_by_float(stack, entering[c])
            for k, s in enumerate(levels):
                value = product[k * full : (k + 1) * full] + (rest[s - 1, c] if s else first[c])
                at = 2 * unknowns * (s * columns + c)
                for h in range(2):
                    half = value[:unknowns, h * LANES : (h + 1) * LANES]
                    out[pl.ds(at + h, unknowns, stride=2), :] = half
        span = pl.ds(part * total // 2, total // 2)
        copies.append(pltpu.make_async_copy(out.at[span], result.at[span], sems.at[part]))
        copies[-1].start()
    for copy in copies:
        copy.wait()


def call(kernel, outs, *args, us, smem=(), scratch=(), kept=0, direct=0):
    vmem, hbm = (pl.BlockSpec(memory_space=space) for space in (pltpu.VMEM, pltpu.HBM))
    away = kept or direct
    near = len(outs) - away

    def with_copies(*refs):
        refs, sems = refs[:-1], refs[-1]
        ins, rest = refs[: len(args)], refs[len(args) :]
        results, far, rest = rest[:near], rest[near : len(outs)], rest[len(outs) :]
        staged, rest = rest[:kept], rest[kept:]
        kernel(*ins, *results, *staged, *rest)
        copies = [
            pltpu.make_async_copy(here, there, sems.at[k])
            for k, (here, there) in enumerate(zip(staged, far))
        ]
        for copy in copies:
            copy.start()
        for copy in copies:
            copy.wait()

    if kept:
        scratch = [pltpu.VMEM(shape, F32) for shape in outs[near:]] + list(scratch)
        scratch.append(pltpu.SemaphoreType.DMA((kept,)))
    return pl.pallas_call(
        with_copies if kept else kernel,
        out_shape=[jax.ShapeDtypeStruct(shape, F32) for shape in outs[:near]]
        + [pltpu.HBM(shape, F32) for shape in outs[near:]],
        in_specs=[
            pl.BlockSpec(memory_space=pltpu.SMEM) if i in smem else vmem for i in range(len(args))
        ],
        out_specs=[vmem] * near + [hbm] * away,
        scratch_shapes=scratch,
        compiler_params=pltpu.CompilerParams(vmem_limit_bytes=28 * 2**20),
        cost_estimate=pl.CostEstimate(
            flops=int(us * 10**9), bytes_accessed=int(us * 10**6), transcendentals=0
        ),
    )(*args)


def shards(source, inv_diag, upstream, downstream, cross_lower, cross_upper):
    positions, columns, planes, unknowns, vectors = source.shape
    squeeze = lambda a: a.reshape(positions, columns, *a.shape[3:])
    source_in = source
    source, inverse, before = squeeze(source), squeeze(inv_diag), squeeze(upstream)
    after, lower, upper = squeeze(downstream), squeeze(cross_lower), squeeze(cross_upper)
    full = -(-unknowns // 8) * 8
    room = full + 8
    fold = (full // 8 + 1) // 2 * 8
    peers = ROW // columns
    count = lax.axis_size("sweep")
    rows = count // ROW
    inside = [[r * ROW + i for i in range(ROW)] for r in range(rows)]
    across = [[r * ROW + i for r in range(rows)] for i in range(ROW)]
    row = (lax.axis_index("sweep") // ROW).astype(jnp.int32).reshape(1)
    ends = lax.axis_size("cross") - 1
    block = (positions, columns, full, vectors)
    others = (positions - 1, columns, full, vectors)
    side = (positions, 2, full, vectors)

    def exchange(x, groups):
        return lax.all_to_all(x, "sweep", 0, 0, axis_index_groups=groups)

    def from_below(x):
        return lax.ppermute(x, "cross", [(i, i + 1) for i in range(ends)])

    def from_above(x):
        return lax.ppermute(x, "cross", [(i + 1, i) for i in range(ends)])

    def settle(backward, joined, states):
        (sent,) = call(
            functools.partial(enter, full, backward),
            [(ROW, fold, LANES)],
            row,
            joined,
            states,
            us=1,
            smem=(0,),
        )
        return exchange(sent, inside)

    (sent,) = call(
        start,
        [(ROW, 2 * room + fold, LANES)],
        inverse,
        before,
        after,
        source,
        us=4,
        direct=1,
        scratch=[
            pltpu.VMEM((columns, 2, room, LANES), F32),
            pltpu.VMEM((columns, peers, full, LANES), F32),
            pltpu.SemaphoreType.DMA((3 * ROW,)),
        ],
    )
    received = exchange(sent, inside)
    *raw, sent = lax.optimization_barrier((inv_diag, upstream, downstream, source_in, sent))
    inverse, before, after, source = map(squeeze, raw)
    ends_sent = (positions, room + 2 * full, LANES)
    first, second, head, tail = call(
        prepare, [ends_sent, ends_sent, side, side], inverse, before, source, us=3, kept=4
    )
    back_maps, back_steps = call(
        compose_back, [block, block], inverse, after, us=2, kept=2
    )
    below, above = from_below(second), from_above(first)
    plan, more = call(
        couple,
        [(columns, 4, full, vectors), (positions - 1, columns, 4, full, vectors)],
        inverse,
        lower,
        upper,
        head,
        tail,
        below,
        above,
        back_steps,
        us=6,
        kept=2,
    )
    received, plan, more = lax.optimization_barrier((received, plan, more))
    (sent,) = call(
        functools.partial(fore_run, full), [(rows, room + fold, LANES)], received, us=1.5
    )
    joined = exchange(sent, across)
    states, later = call(
        functools.partial(fore_prefixes, full),
        [(ROW - 1, full, 2 * LANES), (ROW, room, LANES)],
        received,
        us=2.5,
        direct=1,
        scratch=[pltpu.SemaphoreType.DMA],
    )
    entering = settle(False, joined, states)
    below, above = from_below(entering[peers:]), from_above(entering[:peers])
    (part,) = call(near_part, [(columns, full, vectors)], entering, plan, us=0.6)
    sent, first = call(
        far_part,
        [(ROW, fold, LANES), (columns, full, vectors)],
        below,
        above,
        plan,
        part,
        us=0.6,
    )
    received = exchange(sent, inside)
    received, more = lax.optimization_barrier((received, more))
    (values,) = call(levels, [others], entering, below, above, more, us=3, kept=1)
    order = range(ROW - 1, -1, -1)
    (sent,) = call(
        functools.partial(whole_run, full, order),
        [(rows, room + fold, LANES)],
        later,
        received,
        us=1.5,
    )
    joined = exchange(sent, across)
    (states,) = call(
        functools.partial(prefixes, full, order),
        [(ROW - 1, full, 2 * LANES)],
        later,
        received,
        us=2.5,
    )
    joined, values = lax.optimization_barrier((joined, values))
    entering = settle(True, joined, states)
    lines = positions * columns * unknowns * 2
    (update,) = call(
        finish,
        [(lines, LANES)],
        entering,
        back_maps,
        first,
        values,
        us=2,
        direct=1,
        scratch=[pltpu.VMEM((lines + 16, LANES), F32), pltpu.SemaphoreType.DMA((2,))],
    )
    return update.reshape(positions, columns, planes, unknowns, vectors)


def solution(mesh):
    placed = P("sweep", "cross", None, None, None)
    return jax.shard_map(
        shards,
        mesh=mesh,
        in_specs=(placed,) * 6,
        out_specs=placed,
        check_vma=False,
    )
```

```python
import functools

import jax
import jax.numpy as jnp
from jax import lax
from jax.experimental import pallas as pl
from jax.experimental.pallas import tpu as pltpu
from jax.sharding import PartitionSpec as P

ROW = 8
LANES = 128
F32 = jnp.float32
BF16 = jnp.bfloat16


def halves(x):
    high = x.astype(BF16)
    return high, (x - high.astype(F32)).astype(BF16)


def mul(a, b):
    return jnp.dot(a, b, preferred_element_type=F32)


def exact_by_float(a, b):
    high, low = halves(b)
    return mul(a, high) + mul(a, low)


def float_by_float(a, b):
    a_high, a_low = halves(a)
    b_high, b_low = halves(b)
    return mul(a_high, b_high) + (mul(a_high, b_low) + mul(a_low, b_high))


def lane(shape):
    return lax.broadcasted_iota(jnp.int32, shape, len(shape) - 1)


def put(ref, at, value):
    rows = value.shape[0]
    full = ref.shape[-2]
    tail = full - full % 8 if full % 8 else full - 8
    ref[(*at, slice(tail, full), slice(None))] = jnp.zeros((full - tail, ref.shape[-1]), F32)
    ref[(*at, slice(0, rows), slice(0, value.shape[1]))] = value


def pack_map(matrix, width=7):
    rows = matrix.shape[0]
    strip = jnp.where(lane((rows, LANES)) < width, matrix[:, LANES:], 0.0)
    folded = strip[:8]
    for t in range(1, rows // 8):
        folded = folded + pltpu.roll(strip[8 * t : 8 * t + 8], width * t, 1)
    return jnp.concatenate([matrix[:, :LANES], folded], axis=0)


def unpack_map(block, width=7):
    rows = block.shape[0] - 8
    folded = block[rows:]
    parts = [folded] + [pltpu.roll(folded, LANES - width * t, 1) for t in range(1, rows // 8)]
    strip = jnp.concatenate(parts, axis=0)
    strip = jnp.where(lane(strip.shape) < width, strip, 0.0)
    return jnp.concatenate([block[:rows], strip], axis=1)


def fold_rows(low, high):
    top = (low.shape[0] // 8 + 1) // 2 * 8
    under = jnp.concatenate(
        [high[top:], jnp.zeros((2 * top - high.shape[0], LANES), F32)], axis=0
    )
    return jnp.where(lane((top, LANES)) < 64, low[:top], under)


def pack_slice(pair, odd):
    turned = pltpu.roll(pair, 64, 1)
    return fold_rows(turned, pair) if odd else fold_rows(pair, turned)


def unpack_slice(block, rows, odd):
    turned = pltpu.roll(block, 64, 1)
    first, second = (turned, block) if odd else (block, turned)
    both = jnp.concatenate([first, second[: rows - block.shape[0]]], axis=0)
    keep = lane(both.shape) >= 64 if odd else lane(both.shape) < 64
    return jnp.where(keep, both, 0.0)


def compose(inverse, before, source, fore):
    positions, columns, unknowns, _ = source.shape
    full = fore.shape[-2]
    for s in range(positions):
        for c in range(columns):
            diagonal = inverse[s, c]
            step = -mul(diagonal, before[s, c])
            value = mul(diagonal, source[s, c])
            if s == 0:
                fore[c][s, 0] = jnp.zeros((full, 2 * LANES), F32)
                put(fore[c], (s, 0), step)
                put(fore[c], (s, 1), value)
            else:
                put(fore[c], (s, 0), float_by_float(step, fore[c][s - 1, 0, :unknowns]))
                put(fore[c], (s, 1), value + float_by_float(step, fore[c][s - 1, 1, :unknowns]))


class Pair(tuple):
    @property
    def shape(self):
        return self[0].shape


def compose_back(inverse, after, maps, steps):
    positions, columns = inverse.shape[:2]
    full = maps.shape[-2]
    last = positions - 1
    for s in range(positions):
        for c in range(columns):
            steps[s, c] = jnp.zeros((full, 2 * LANES), F32)
            put(steps, (s, c), -mul(inverse[s, c], after[s, c]))
    for c in range(columns):
        maps[last, c] = steps[last, c]
    for s in range(last - 1, -1, -1):
        for c in range(columns):
            maps[s, c] = float_by_float(steps[s, c, :, :full], maps[s + 1, c])


PIECES = 2


def piece_rows(full):
    return -(-(full + 8) // (8 * PIECES)) * 8


def start(inverse, before, after, source, sent, maps, values, sems):
    positions, columns, unknowns, vectors = source.shape
    full = values.shape[-2]
    room = full + 8
    peers = ROW // columns
    piece = piece_rows(full)
    copies = []

    def send(ref, at, low):
        there = sent.at[at, pl.ds(low, ref.shape[0])]
        copies.append(pltpu.make_async_copy(ref, there, sems.at[len(copies)]))
        copies[-1].start()

    def padded(value):
        rows, lanes = full - value.shape[0], 2 * LANES - value.shape[1]
        return jnp.pad(value, ((0, rows), (0, lanes)))

    for c in range(columns):
        steps = [-mul(inverse[s, c], after[s, c]) for s in range(positions)]
        while len(steps) > 1:
            steps = [float_by_float(*steps[k : k + 2]) for k in range(0, len(steps), 2)]
        maps[c, 1] = pack_map(padded(steps[0]))
        for q in range(peers):
            send(maps.at[c, 1, pl.ds(q % PIECES * piece, piece)], c * peers + q, room)
    for c in range(columns):
        steps = [
            (-mul(inverse[s, c], before[s, c]), mul(inverse[s, c], source[s, c]))
            for s in range(positions)
        ]
        while len(steps) > 1:
            steps = [
                (float_by_float(later[0], earlier[0]), later[1] + float_by_float(later[0], earlier[1]))
                for earlier, later in zip(steps[::2], steps[1::2])
            ]
        maps[c, 0] = pack_map(padded(steps[0][0]))
        value = padded(steps[0][1])
        for q in range(peers):
            send(maps.at[c, 0], c * peers + q, 0)
            pair = value[:, q // 2 * LANES : (q // 2 + 1) * LANES]
            fold = (full // 8 + 1) // 2 * 8
            values[c, q, 0:fold] = pack_slice(pair, q % 2)
            send(values.at[c, q, pl.ds(0, fold)], c * peers + q, room + piece)
    for copy in copies:
        copy.wait()


def prepare(inverse, before, source, first, second, head, tail):
    positions, columns = source.shape[:2]
    full = head.shape[-2]
    room = full + 8
    compose(inverse, before, source, Pair((head, tail)))
    for fore, sent in ((head, first), (tail, second)):
        for s in range(positions):
            sent[s, 0:room] = pack_map(fore[s, 0])
            sent[s, room : room + full] = fore[s, 1, :, :LANES]
            sent[s, room + full :] = fore[s, 1, :, LANES:]


def ship_row(full, state, sent):
    block = jnp.concatenate([pack_map(state), pack_slice(state[:, LANES:], 1)], axis=0)
    for x in range(sent.shape[0]):
        sent[x] = block


def unpack_step(full, matrix, block):
    value = unpack_slice(block, full, 1)
    return unpack_map(matrix) + jnp.concatenate([jnp.zeros_like(value), value], axis=1)


def follow(full, earlier, later):
    product = float_by_float(later[:, :full], earlier)
    kept = lane((full, LANES)) >= 64
    value = jnp.where(kept, later[:, LANES:], 0.0)
    return product + jnp.concatenate([jnp.zeros_like(value), value], axis=1)


def whole_run(full, order, matrices, blocks, sent):
    steps = [unpack_step(full, matrices[d], blocks[d]) for d in order]
    while len(steps) > 1:
        steps = [follow(full, *steps[k : k + 2]) for k in range(0, len(steps), 2)]
    ship_row(full, steps[0], sent)


def prefixes(full, order, matrices, blocks, states):
    state = None
    for k, d in enumerate(order[: states.shape[0]]):
        step = unpack_step(full, matrices[d], blocks[d])
        state = step if state is None else follow(full, state, step)
        states[k] = state


def fore_views(full, received):
    room = full + 8
    fold = (full // 8 + 1) // 2 * 8
    return received.at[:, 0:room], received.at[:, received.shape[1] - fold :]


def fore_run(full, received, piece, sent):
    room = full + 8
    piece[...] = received[:, room : room + piece.shape[1]]
    whole_run(full, range(ROW), *fore_views(full, received), sent)


def fore_prefixes(full, received, states):
    prefixes(full, range(ROW), *fore_views(full, received), states)


def fore_enter(full, row, place, own, other, joined, states, sent, later, sems):
    rows = own.shape[1]
    copies = []
    for d, block in enumerate((own, other)):
        at = pl.multiple_of((place[0] + d) % PIECES * rows, 8)
        copies.append(pltpu.make_async_copy(block, later.at[:, pl.ds(at, rows)], sems.at[d]))
        copies[-1].start()
    enter(full, False, row, joined, states, sent)
    for copy in copies:
        copy.wait()


def enter(full, backward, row, received, states, sent):
    rows = received.shape[0]
    room = full + 8
    order = list(range(rows - 1, 0, -1)) if backward else list(range(rows - 1))
    mine = row[0]
    value = None
    found = jnp.zeros((full, LANES), F32)
    for x in order:
        piece = unpack_slice(received[x, room:], full, 0)
        if value is not None:
            matrix = unpack_map(received[x, 0:room])
            piece = float_by_float(matrix[:, :full], value) + piece
        value = piece
        found = jnp.where(mine == (x - 1 if backward else x + 1), value, found)
    high = found.astype(BF16).astype(F32)
    low = found - high
    under = jnp.zeros((2 * LANES - 64 - full, LANES), F32)
    corner = (
        lax.broadcasted_iota(jnp.int32, (64, LANES), 0) == lane((64, LANES))
    ).astype(F32)
    top = jnp.concatenate([high, under, corner], axis=0)
    bottom = jnp.concatenate([low, under, jnp.zeros((64, LANES), F32)], axis=0)
    both = (top + pltpu.roll(bottom, 64, 1)).astype(BF16)
    stack = states[...].reshape((ROW - 1) * full, 2 * LANES)
    s_high, s_low = halves(stack)
    first = mul(s_high, both)
    every = first + (pltpu.roll(first, 64, 1) + mul(s_low, top.astype(BF16)))
    sent[ROW - 1 if backward else 0] = pack_slice(found, 0)
    for k in range(ROW - 1):
        at = ROW - 2 - k if backward else k + 1
        sent[at] = pack_slice(every[k * full : (k + 1) * full], 0)


def unpack_columns(full, received, first, count):
    parts = []
    for h in range(count // 2):
        at = first + 2 * h
        parts.append(
            unpack_slice(received[at], full, 0)
            + pltpu.roll(unpack_slice(received[at + 1], full, 0), 64, 1)
        )
    return jnp.concatenate(parts, axis=1)


def couple(inverse, lower, upper, head, tail, steps, plan, more):
    positions, columns, unknowns, _ = inverse.shape
    forward = (head, tail)

    def parts(s, c):
        near = upper if c == 0 else lower
        by_near = mul(inverse[s, c], near[s, c])
        return [
            forward[c][s, 0, :unknowns],
            -float_by_float(by_near, forward[1 - c][s, 0, :unknowns]),
            forward[c][s, 1, :unknowns]
            - float_by_float(by_near, forward[1 - c][s, 1, :unknowns]),
        ]

    accumulate(parts, steps, unknowns, plan, more)


def couple_far(inverse, lower, upper, below, above, steps, plan, more):
    positions, columns, unknowns, _ = inverse.shape
    full = plan.shape[-2]
    room = full + 8
    halo = (below, above)

    def parts(s, c):
        far = lower if c == 0 else upper
        by_far = -mul(inverse[s, c], far[s, c])
        value = jnp.concatenate(
            [halo[c][s, room : room + full], halo[c][s, room + full :]], axis=1
        )
        return [
            float_by_float(by_far, unpack_map(halo[c][s, 0:room])[:unknowns]),
            float_by_float(by_far, value[:unknowns]),
        ]

    accumulate(parts, steps, unknowns, plan, more)


def accumulate(parts, steps, unknowns, plan, more):
    for c in range(plan.shape[0]):
        kept = None
        for s in range(more.shape[0], -1, -1):
            new = parts(s, c)
            if kept is not None:
                step = steps[s, c, :unknowns, :unknowns]
                new = [part + float_by_float(step, old) for part, old in zip(new, kept)]
            kept = new
            for k, value in enumerate(kept):
                put(*((plan, (c, k)) if s == 0 else (more, (s - 1, c, k))), value)


def near_part(received, plan, far_plan, part):
    columns, full, _ = part.shape
    peers = ROW // columns
    entering = [unpack_columns(full, received, c * peers, peers) for c in range(columns)]
    for c in range(columns):
        part[c] = (plan[c, 2] + far_plan[c, 1]) + (
            float_by_float(plan[c, 0, :, :full], entering[c])
            + float_by_float(plan[c, 1, :, :full], entering[1 - c])
        )


def far_part(below, above, plan, part, sent, values):
    columns, full, _ = part.shape
    peers = ROW // columns
    halo = (below, above)
    for c in range(columns):
        entering = unpack_columns(full, halo[c], 0, peers)
        value = part[c] + float_by_float(plan[c, 0, :, :full], entering)
        values[c] = value
        for q in range(peers):
            pair = value[:, q // 2 * LANES : (q // 2 + 1) * LANES]
            sent[c * peers + q] = pack_slice(pair, q % 2)


def levels(received, below, above, more, far_more, values):
    others, columns, full, _ = values.shape
    peers = ROW // columns
    entering = [unpack_columns(full, received, c * peers, peers) for c in range(columns)]
    halo = [unpack_columns(full, got, 0, peers) for got in (below, above)]
    for c in range(columns):
        total = None
        for maps, k, value in (
            (more, 0, entering[c]),
            (more, 1, entering[1 - c]),
            (far_more, 0, halo[c]),
        ):
            stack = jnp.concatenate([maps[s, c, k, :, :full] for s in range(others)], axis=0)
            product = float_by_float(stack, value)
            total = product if total is None else total + product
        for s in range(others):
            value = more[s, c, 2] + far_more[s, c, 1]
            values[s, c] = value + total[s * full : (s + 1) * full]


def finish(received, maps, first, rest, result, out, sems):
    positions, columns, full, vectors = maps.shape
    peers = ROW // columns
    total = result.shape[0]
    unknowns = total // (2 * positions * columns)
    entering = [unpack_columns(full, received, c * peers, peers) for c in range(columns)]
    copies = []
    for part in range(2):
        levels = range(part * positions // 2, (part + 1) * positions // 2)
        for c in range(columns):
            stack = jnp.concatenate([maps[s, c, :, :full] for s in levels], axis=0)
            product = float_by_float(stack, entering[c])
            for k, s in enumerate(levels):
                value = product[k * full : (k + 1) * full] + (rest[s - 1, c] if s else first[c])
                at = 2 * unknowns * (s * columns + c)
                for h in range(2):
                    half = value[:unknowns, h * LANES : (h + 1) * LANES]
                    out[pl.ds(at + h, unknowns, stride=2), :] = half
        span = pl.ds(part * total // 2, total // 2)
        copies.append(pltpu.make_async_copy(out.at[span], result.at[span], sems.at[part]))
        copies[-1].start()
    for copy in copies:
        copy.wait()


def call(kernel, outs, *args, us, smem=(), scratch=(), kept=0, direct=0):
    vmem, hbm = (pl.BlockSpec(memory_space=space) for space in (pltpu.VMEM, pltpu.HBM))
    away = kept or direct
    near = len(outs) - away

    def with_copies(*refs):
        refs, sems = refs[:-1], refs[-1]
        ins, rest = refs[: len(args)], refs[len(args) :]
        results, far, rest = rest[:near], rest[near : len(outs)], rest[len(outs) :]
        staged, rest = rest[:kept], rest[kept:]
        kernel(*ins, *results, *staged, *rest)
        copies = [
            pltpu.make_async_copy(here, there, sems.at[k])
            for k, (here, there) in enumerate(zip(staged, far))
        ]
        for copy in copies:
            copy.start()
        for copy in copies:
            copy.wait()

    if kept:
        scratch = [pltpu.VMEM(shape, F32) for shape in outs[near:]] + list(scratch)
        scratch.append(pltpu.SemaphoreType.DMA((kept,)))
    return pl.pallas_call(
        with_copies if kept else kernel,
        out_shape=[jax.ShapeDtypeStruct(shape, F32) for shape in outs[:near]]
        + [pltpu.HBM(shape, F32) for shape in outs[near:]],
        in_specs=[
            pl.BlockSpec(memory_space=pltpu.SMEM) if i in smem else vmem for i in range(len(args))
        ],
        out_specs=[vmem] * near + [hbm] * away,
        scratch_shapes=scratch,
        compiler_params=pltpu.CompilerParams(vmem_limit_bytes=28 * 2**20),
        cost_estimate=pl.CostEstimate(
            flops=int(us * 10**9), bytes_accessed=int(us * 10**6), transcendentals=0
        ),
    )(*args)


def shards(source, inv_diag, upstream, downstream, cross_lower, cross_upper):
    positions, columns, planes, unknowns, vectors = source.shape
    squeeze = lambda a: a.reshape(positions, columns, *a.shape[3:])
    source_in = source
    source, inverse, before = squeeze(source), squeeze(inv_diag), squeeze(upstream)
    after, lower, upper = squeeze(downstream), squeeze(cross_lower), squeeze(cross_upper)
    full = -(-unknowns // 8) * 8
    room = full + 8
    fold = (full // 8 + 1) // 2 * 8
    peers = ROW // columns
    piece = piece_rows(full)
    place = (lax.axis_index("sweep") % ROW).astype(jnp.int32).reshape(1)
    count = lax.axis_size("sweep")
    rows = count // ROW
    inside = [[r * ROW + i for i in range(ROW)] for r in range(rows)]
    across = [[r * ROW + i for r in range(rows)] for i in range(ROW)]
    row = (lax.axis_index("sweep") // ROW).astype(jnp.int32).reshape(1)
    ends = lax.axis_size("cross") - 1
    block = (positions, columns, full, vectors)
    others = (positions - 1, columns, full, vectors)
    side = (positions, 2, full, vectors)

    def exchange(x, groups):
        return lax.all_to_all(x, "sweep", 0, 0, axis_index_groups=groups)

    def from_below(x):
        return lax.ppermute(x, "cross", [(i, i + 1) for i in range(ends)])

    def from_above(x):
        return lax.ppermute(x, "cross", [(i + 1, i) for i in range(ends)])

    (sent,) = call(
        start,
        [(ROW, room + piece + fold, LANES)],
        inverse,
        before,
        after,
        source,
        us=4,
        direct=1,
        scratch=[
            pltpu.VMEM((columns, 2, room, LANES), F32),
            pltpu.VMEM((columns, peers, full, LANES), F32),
            pltpu.SemaphoreType.DMA((3 * ROW,)),
        ],
    )
    received = exchange(sent, inside)
    *raw, sent = lax.optimization_barrier((inv_diag, upstream, downstream, source_in, sent))
    inverse, before, after, source = map(squeeze, raw)
    ends_sent = (positions, room + 2 * full, LANES)
    first, second, head, tail = call(
        prepare, [ends_sent, ends_sent, side, side], inverse, before, source, us=3, kept=4
    )
    back_maps, back_steps = call(
        compose_back, [block, block], inverse, after, us=2, kept=2
    )
    below, above = from_below(second), from_above(first)
    plan, more = call(
        couple,
        [(columns, 3, full, vectors), (positions - 1, columns, 3, full, vectors)],
        inverse,
        lower,
        upper,
        head,
        tail,
        back_steps,
        us=4,
        kept=2,
    )
    far_plan, far_more = call(
        couple_far,
        [(columns, 2, full, vectors), (positions - 1, columns, 2, full, vectors)],
        inverse,
        lower,
        upper,
        below,
        above,
        back_steps,
        us=3,
        kept=2,
    )
    received, plan, more, far_plan, far_more = lax.optimization_barrier(
        (received, plan, more, far_plan, far_more)
    )
    own, sent = call(
        functools.partial(fore_run, full),
        [(ROW, piece, LANES), (rows, room + fold, LANES)],
        received,
        us=1.5,
    )

    joined = exchange(sent, across)
    other = lax.ppermute(own, "sweep", [(i, i ^ 1) for i in range(count)])
    (states,) = call(
        functools.partial(fore_prefixes, full),
        [(ROW - 1, full, 2 * LANES)],
        received,
        us=2,
    )
    sent, later = call(
        functools.partial(fore_enter, full),
        [(ROW, fold, LANES), (ROW, room, LANES)],
        row,
        place,
        own,
        other,
        joined,
        states,
        us=1,
        smem=(0, 1),
        direct=1,
        scratch=[pltpu.SemaphoreType.DMA((PIECES,))],
    )
    entering = exchange(sent, inside)
    below, above = from_below(entering[peers:]), from_above(entering[:peers])
    (part,) = call(near_part, [(columns, full, vectors)], entering, plan, far_plan, us=0.6)
    sent, first = call(
        far_part,
        [(ROW, fold, LANES), (columns, full, vectors)],
        below,
        above,
        far_plan,
        part,
        us=0.6,
    )
    received = exchange(sent, inside)
    received, more = lax.optimization_barrier((received, more))
    (values,) = call(levels, [others], entering, below, above, more, far_more, us=3, kept=1)
    order = range(ROW - 1, -1, -1)
    (sent,) = call(
        functools.partial(whole_run, full, order),
        [(rows, room + fold, LANES)],
        later,
        received,
        us=1.5,
    )
    joined = exchange(sent, across)
    (states,) = call(
        functools.partial(prefixes, full, order),
        [(ROW - 1, full, 2 * LANES)],
        later,
        received,
        us=2.5,
    )
    joined, values = lax.optimization_barrier((joined, values))
    (sent,) = call(
        functools.partial(enter, full, True),
        [(ROW, fold, LANES)],
        row,
        joined,
        states,
        us=1,
        smem=(0,),
    )
    entering = exchange(sent, inside)
    lines = positions * columns * unknowns * 2
    (update,) = call(
        finish,
        [(lines, LANES)],
        entering,
        back_maps,
        first,
        values,
        us=2,
        direct=1,
        scratch=[pltpu.VMEM((lines + 16, LANES), F32), pltpu.SemaphoreType.DMA((2,))],
    )
    return update.reshape(positions, columns, planes, unknowns, vectors)


def solution(mesh):
    placed = P("sweep", "cross", None, None, None)
    return jax.shard_map(
        shards,
        mesh=mesh,
        in_specs=(placed,) * 6,
        out_specs=placed,
        check_vma=False,
    )
```

```python
import functools

import jax
import jax.numpy as jnp
from jax import lax
from jax.experimental import pallas as pl
from jax.experimental.pallas import tpu as pltpu
from jax.sharding import PartitionSpec as P

ROW = 8
LANES = 128
F32 = jnp.float32
BF16 = jnp.bfloat16


def halves(x):
    high = x.astype(BF16)
    return high, (x - high.astype(F32)).astype(BF16)


def mul(a, b):
    return jnp.dot(a, b, preferred_element_type=F32)


def exact_by_float(a, b):
    high, low = halves(b)
    return mul(a, high) + mul(a, low)


def float_by_float(a, b):
    a_high, a_low = halves(a)
    b_high, b_low = halves(b)
    return mul(a_high, b_high) + (mul(a_high, b_low) + mul(a_low, b_high))


def lane(shape):
    return lax.broadcasted_iota(jnp.int32, shape, len(shape) - 1)


def put(ref, at, value):
    rows = value.shape[0]
    full = ref.shape[-2]
    tail = full - full % 8 if full % 8 else full - 8
    ref[(*at, slice(tail, full), slice(None))] = jnp.zeros((full - tail, ref.shape[-1]), F32)
    ref[(*at, slice(0, rows), slice(0, value.shape[1]))] = value


def pack_map(matrix, width=7):
    rows = matrix.shape[0]
    strip = jnp.where(lane((rows, LANES)) < width, matrix[:, LANES:], 0.0)
    folded = strip[:8]
    for t in range(1, rows // 8):
        folded = folded + pltpu.roll(strip[8 * t : 8 * t + 8], width * t, 1)
    return jnp.concatenate([matrix[:, :LANES], folded], axis=0)


def unpack_map(block, width=7):
    rows = block.shape[0] - 8
    folded = block[rows:]
    parts = [folded] + [pltpu.roll(folded, LANES - width * t, 1) for t in range(1, rows // 8)]
    strip = jnp.concatenate(parts, axis=0)
    strip = jnp.where(lane(strip.shape) < width, strip, 0.0)
    return jnp.concatenate([block[:rows], strip], axis=1)


def fold_rows(low, high):
    top = (low.shape[0] // 8 + 1) // 2 * 8
    under = jnp.concatenate(
        [high[top:], jnp.zeros((2 * top - high.shape[0], LANES), F32)], axis=0
    )
    return jnp.where(lane((top, LANES)) < 64, low[:top], under)


def pack_slice(pair, odd):
    turned = pltpu.roll(pair, 64, 1)
    return fold_rows(turned, pair) if odd else fold_rows(pair, turned)


def unpack_slice(block, rows, odd):
    turned = pltpu.roll(block, 64, 1)
    first, second = (turned, block) if odd else (block, turned)
    both = jnp.concatenate([first, second[: rows - block.shape[0]]], axis=0)
    keep = lane(both.shape) >= 64 if odd else lane(both.shape) < 64
    return jnp.where(keep, both, 0.0)


def compose(inverse, before, source, fore):
    positions, columns, unknowns, _ = source.shape
    full = fore.shape[-2]
    for s in range(positions):
        for c in range(columns):
            diagonal = inverse[s, c]
            step = -mul(diagonal, before[s, c])
            value = mul(diagonal, source[s, c])
            if s == 0:
                fore[c][s, 0] = jnp.zeros((full, 2 * LANES), F32)
                put(fore[c], (s, 0), step)
                put(fore[c], (s, 1), value)
            else:
                put(fore[c], (s, 0), float_by_float(step, fore[c][s - 1, 0, :unknowns]))
                put(fore[c], (s, 1), value + float_by_float(step, fore[c][s - 1, 1, :unknowns]))


class Pair(tuple):
    @property
    def shape(self):
        return self[0].shape


def compose_back(inverse, after, maps, steps):
    positions, columns = inverse.shape[:2]
    full = maps.shape[-2]
    last = positions - 1
    for s in range(positions):
        for c in range(columns):
            steps[s, c] = jnp.zeros((full, 2 * LANES), F32)
            put(steps, (s, c), -mul(inverse[s, c], after[s, c]))
    for c in range(columns):
        maps[last, c] = steps[last, c]
    for s in range(last - 1, -1, -1):
        for c in range(columns):
            maps[s, c] = float_by_float(steps[s, c, :, :full], maps[s + 1, c])


PIECES = 2


def piece_rows(full):
    return -(-(full + 8) // (8 * PIECES)) * 8


def start(turn, inverse, before, after, source, sent, maps, values, sems):
    positions, columns, unknowns, vectors = source.shape
    full = values.shape[-2]
    room = full + 8
    peers = ROW // columns
    piece = piece_rows(full)
    copies = []

    def send(ref, at, low):
        there = sent.at[(turn[0] + at) % ROW, pl.ds(low, ref.shape[0])]
        copies.append(pltpu.make_async_copy(ref, there, sems.at[len(copies)]))
        copies[-1].start()

    def padded(value):
        rows, lanes = full - value.shape[0], 2 * LANES - value.shape[1]
        return jnp.pad(value, ((0, rows), (0, lanes)))

    for c in range(columns):
        steps = [-mul(inverse[s, c], after[s, c]) for s in range(positions)]
        while len(steps) > 1:
            steps = [float_by_float(*steps[k : k + 2]) for k in range(0, len(steps), 2)]
        maps[c, 1] = pack_map(padded(steps[0]))
        for q in range(peers):
            send(maps.at[c, 1, pl.ds(q % PIECES * piece, piece)], c * peers + q, room)
    for c in range(columns):
        steps = [
            (-mul(inverse[s, c], before[s, c]), mul(inverse[s, c], source[s, c]))
            for s in range(positions)
        ]
        while len(steps) > 1:
            steps = [
                (float_by_float(later[0], earlier[0]), later[1] + float_by_float(later[0], earlier[1]))
                for earlier, later in zip(steps[::2], steps[1::2])
            ]
        maps[c, 0] = pack_map(padded(steps[0][0]))
        value = padded(steps[0][1])
        for q in range(peers):
            send(maps.at[c, 0], c * peers + q, 0)
            pair = value[:, q // 2 * LANES : (q // 2 + 1) * LANES]
            fold = (full // 8 + 1) // 2 * 8
            values[c, q, 0:fold] = pack_slice(pair, q % 2)
            send(values.at[c, q, pl.ds(0, fold)], c * peers + q, room + piece)
    for copy in copies:
        copy.wait()


def prepare(inverse, before, source, first, second, head, tail):
    positions, columns = source.shape[:2]
    full = head.shape[-2]
    room = full + 8
    compose(inverse, before, source, Pair((head, tail)))
    for fore, sent in ((head, first), (tail, second)):
        for s in range(positions):
            sent[s, 0:room] = pack_map(fore[s, 0])
            sent[s, room : room + full] = fore[s, 1, :, :LANES]
            sent[s, room + full :] = fore[s, 1, :, LANES:]


def ship_row(full, state, sent):
    block = jnp.concatenate([pack_map(state), pack_slice(state[:, LANES:], 1)], axis=0)
    for x in range(sent.shape[0]):
        sent[x] = block


def unpack_step(full, matrix, block):
    value = unpack_slice(block, full, 1)
    return unpack_map(matrix) + jnp.concatenate([jnp.zeros_like(value), value], axis=1)


def follow(full, earlier, later):
    product = float_by_float(later[:, :full], earlier)
    kept = lane((full, LANES)) >= 64
    value = jnp.where(kept, later[:, LANES:], 0.0)
    return product + jnp.concatenate([jnp.zeros_like(value), value], axis=1)


def whole_run(full, order, matrices, blocks, sent):
    steps = [unpack_step(full, matrices[d], blocks[d]) for d in order]
    while len(steps) > 1:
        steps = [follow(full, *steps[k : k + 2]) for k in range(0, len(steps), 2)]
    ship_row(full, steps[0], sent)


def prefixes(full, order, matrices, blocks, states):
    state = None
    for k, d in enumerate(order[: states.shape[0]]):
        step = unpack_step(full, matrices[d], blocks[d])
        state = step if state is None else follow(full, state, step)
        states[k] = state


def fore_views(full, received):
    room = full + 8
    fold = (full // 8 + 1) // 2 * 8
    return received.at[:, 0:room], received.at[:, received.shape[1] - fold :]


def fore_run(full, received, piece, sent):
    room = full + 8
    piece[...] = received[:, room : room + piece.shape[1]]
    whole_run(full, range(ROW), *fore_views(full, received), sent)


def fore_prefixes(full, received, states):
    prefixes(full, range(ROW), *fore_views(full, received), states)


def fore_enter(full, row, place, own, other, joined, states, sent, later, sems):
    rows = own.shape[1]
    copies = []
    for d, block in enumerate((own, other)):
        at = pl.multiple_of((place[0] + d) % PIECES * rows, 8)
        copies.append(pltpu.make_async_copy(block, later.at[:, pl.ds(at, rows)], sems.at[d]))
        copies[-1].start()
    enter(full, False, row, joined, states, sent)
    for copy in copies:
        copy.wait()


def enter(full, backward, row, received, states, sent):
    rows = received.shape[0]
    room = full + 8
    order = list(range(rows - 1, 0, -1)) if backward else list(range(rows - 1))
    mine = row[0]
    value = None
    found = jnp.zeros((full, LANES), F32)
    for x in order:
        piece = unpack_slice(received[x, room:], full, 0)
        if value is not None:
            matrix = unpack_map(received[x, 0:room])
            piece = float_by_float(matrix[:, :full], value) + piece
        value = piece
        found = jnp.where(mine == (x - 1 if backward else x + 1), value, found)
    high = found.astype(BF16).astype(F32)
    low = found - high
    under = jnp.zeros((2 * LANES - 64 - full, LANES), F32)
    corner = (
        lax.broadcasted_iota(jnp.int32, (64, LANES), 0) == lane((64, LANES))
    ).astype(F32)
    top = jnp.concatenate([high, under, corner], axis=0)
    bottom = jnp.concatenate([low, under, jnp.zeros((64, LANES), F32)], axis=0)
    both = (top + pltpu.roll(bottom, 64, 1)).astype(BF16)
    stack = states[...].reshape((ROW - 1) * full, 2 * LANES)
    s_high, s_low = halves(stack)
    first = mul(s_high, both)
    every = first + (pltpu.roll(first, 64, 1) + mul(s_low, top.astype(BF16)))
    sent[ROW - 1 if backward else 0] = pack_slice(found, 0)
    for k in range(ROW - 1):
        at = ROW - 2 - k if backward else k + 1
        sent[at] = pack_slice(every[k * full : (k + 1) * full], 0)


def unpack_columns(full, received, first, count, turn=None):
    def block(at):
        return received[at if turn is None else (turn[0] + at) % ROW]

    parts = []
    for h in range(count // 2):
        at = first + 2 * h
        parts.append(
            unpack_slice(block(at), full, 0)
            + pltpu.roll(unpack_slice(block(at + 1), full, 0), 64, 1)
        )
    return jnp.concatenate(parts, axis=1)


def couple(inverse, lower, upper, head, tail, steps, plan, more):
    positions, columns, unknowns, _ = inverse.shape
    forward = (head, tail)

    def parts(s, c):
        near = upper if c == 0 else lower
        by_near = mul(inverse[s, c], near[s, c])
        return [
            forward[c][s, 0, :unknowns],
            -float_by_float(by_near, forward[1 - c][s, 0, :unknowns]),
            forward[c][s, 1, :unknowns]
            - float_by_float(by_near, forward[1 - c][s, 1, :unknowns]),
        ]

    accumulate(parts, steps, unknowns, plan, more)


def couple_far(inverse, lower, upper, below, above, steps, plan, more):
    positions, columns, unknowns, _ = inverse.shape
    full = plan.shape[-2]
    room = full + 8
    halo = (below, above)

    def parts(s, c):
        far = lower if c == 0 else upper
        by_far = -mul(inverse[s, c], far[s, c])
        value = jnp.concatenate(
            [halo[c][s, room : room + full], halo[c][s, room + full :]], axis=1
        )
        return [
            float_by_float(by_far, unpack_map(halo[c][s, 0:room])[:unknowns]),
            float_by_float(by_far, value[:unknowns]),
        ]

    accumulate(parts, steps, unknowns, plan, more)


def accumulate(parts, steps, unknowns, plan, more):
    for c in range(plan.shape[0]):
        kept = None
        for s in range(more.shape[0], -1, -1):
            new = parts(s, c)
            if kept is not None:
                step = steps[s, c, :unknowns, :unknowns]
                new = [part + float_by_float(step, old) for part, old in zip(new, kept)]
            kept = new
            for k, value in enumerate(kept):
                put(*((plan, (c, k)) if s == 0 else (more, (s - 1, c, k))), value)


def by_column(turn, received, *outs):
    for c, out in enumerate(outs):
        peers = out.shape[0]
        for q in range(peers):
            out[q] = received[(turn[0] + c * peers + q) % ROW]


def near_part(turn, received, plan, far_plan, part):
    columns, full, _ = part.shape
    peers = ROW // columns
    entering = [unpack_columns(full, received, c * peers, peers, turn) for c in range(columns)]
    for c in range(columns):
        part[c] = (plan[c, 2] + far_plan[c, 1]) + (
            float_by_float(plan[c, 0, :, :full], entering[c])
            + float_by_float(plan[c, 1, :, :full], entering[1 - c])
        )


def far_part(turn, below, above, plan, part, sent, values):
    columns, full, _ = part.shape
    peers = ROW // columns
    halo = (below, above)
    for c in range(columns):
        entering = unpack_columns(full, halo[c], 0, peers)
        value = part[c] + float_by_float(plan[c, 0, :, :full], entering)
        values[c] = value
        for q in range(peers):
            pair = value[:, q // 2 * LANES : (q // 2 + 1) * LANES]
            sent[(turn[0] + c * peers + q) % ROW] = pack_slice(pair, q % 2)


def levels(turn, received, below, above, more, far_more, values):
    others, columns, full, _ = values.shape
    peers = ROW // columns
    entering = [unpack_columns(full, received, c * peers, peers, turn) for c in range(columns)]
    halo = [unpack_columns(full, got, 0, peers) for got in (below, above)]
    for c in range(columns):
        total = None
        for maps, k, value in (
            (more, 0, entering[c]),
            (more, 1, entering[1 - c]),
            (far_more, 0, halo[c]),
        ):
            stack = jnp.concatenate([maps[s, c, k, :, :full] for s in range(others)], axis=0)
            product = float_by_float(stack, value)
            total = product if total is None else total + product
        for s in range(others):
            value = more[s, c, 2] + far_more[s, c, 1]
            values[s, c] = value + total[s * full : (s + 1) * full]


def finish(turn, received, maps, first, rest, result, out, sems):
    positions, columns, full, vectors = maps.shape
    peers = ROW // columns
    total = result.shape[0]
    unknowns = total // (2 * positions * columns)
    entering = [unpack_columns(full, received, c * peers, peers, turn) for c in range(columns)]
    copies = []
    for part in range(2):
        levels = range(part * positions // 2, (part + 1) * positions // 2)
        for c in range(columns):
            stack = jnp.concatenate([maps[s, c, :, :full] for s in levels], axis=0)
            product = float_by_float(stack, entering[c])
            for k, s in enumerate(levels):
                value = product[k * full : (k + 1) * full] + (rest[s - 1, c] if s else first[c])
                at = 2 * unknowns * (s * columns + c)
                for h in range(2):
                    half = value[:unknowns, h * LANES : (h + 1) * LANES]
                    out[pl.ds(at + h, unknowns, stride=2), :] = half
        span = pl.ds(part * total // 2, total // 2)
        copies.append(pltpu.make_async_copy(out.at[span], result.at[span], sems.at[part]))
        copies[-1].start()
    for copy in copies:
        copy.wait()


def call(kernel, outs, *args, us, smem=(), scratch=(), kept=0, direct=0):
    vmem, hbm = (pl.BlockSpec(memory_space=space) for space in (pltpu.VMEM, pltpu.HBM))
    away = kept or direct
    near = len(outs) - away

    def with_copies(*refs):
        refs, sems = refs[:-1], refs[-1]
        ins, rest = refs[: len(args)], refs[len(args) :]
        results, far, rest = rest[:near], rest[near : len(outs)], rest[len(outs) :]
        staged, rest = rest[:kept], rest[kept:]
        kernel(*ins, *results, *staged, *rest)
        copies = [
            pltpu.make_async_copy(here, there, sems.at[k])
            for k, (here, there) in enumerate(zip(staged, far))
        ]
        for copy in copies:
            copy.start()
        for copy in copies:
            copy.wait()

    if kept:
        scratch = [pltpu.VMEM(shape, F32) for shape in outs[near:]] + list(scratch)
        scratch.append(pltpu.SemaphoreType.DMA((kept,)))
    return pl.pallas_call(
        with_copies if kept else kernel,
        out_shape=[jax.ShapeDtypeStruct(shape, F32) for shape in outs[:near]]
        + [pltpu.HBM(shape, F32) for shape in outs[near:]],
        in_specs=[
            pl.BlockSpec(memory_space=pltpu.SMEM) if i in smem else vmem for i in range(len(args))
        ],
        out_specs=[vmem] * near + [hbm] * away,
        scratch_shapes=scratch,
        compiler_params=pltpu.CompilerParams(vmem_limit_bytes=28 * 2**20),
        cost_estimate=pl.CostEstimate(
            flops=int(us * 10**9), bytes_accessed=int(us * 10**6), transcendentals=0
        ),
    )(*args)


def shards(source, inv_diag, upstream, downstream, cross_lower, cross_upper):
    positions, columns, planes, unknowns, vectors = source.shape
    squeeze = lambda a: a.reshape(positions, columns, *a.shape[3:])
    source_in = source
    source, inverse, before = squeeze(source), squeeze(inv_diag), squeeze(upstream)
    after, lower, upper = squeeze(downstream), squeeze(cross_lower), squeeze(cross_upper)
    full = -(-unknowns // 8) * 8
    room = full + 8
    fold = (full // 8 + 1) // 2 * 8
    peers = ROW // columns
    piece = piece_rows(full)
    turn = (lax.axis_index("cross") % 2).astype(jnp.int32).reshape(1)
    place = (lax.axis_index("sweep").astype(jnp.int32).reshape(1) + ROW - turn) % ROW
    count = lax.axis_size("sweep")
    rows = count // ROW
    inside = [[r * ROW + i for i in range(ROW)] for r in range(rows)]
    across = [[r * ROW + i for r in range(rows)] for i in range(ROW)]
    row = (lax.axis_index("sweep") // ROW).astype(jnp.int32).reshape(1)
    ends = lax.axis_size("cross") - 1
    block = (positions, columns, full, vectors)
    others = (positions - 1, columns, full, vectors)
    side = (positions, 2, full, vectors)

    def exchange(x, groups):
        return lax.all_to_all(x, "sweep", 0, 0, axis_index_groups=groups)

    def from_below(x):
        return lax.ppermute(x, "cross", [(i, i + 1) for i in range(ends)])

    def from_above(x):
        return lax.ppermute(x, "cross", [(i + 1, i) for i in range(ends)])

    (sent,) = call(
        start,
        [(ROW, room + piece + fold, LANES)],
        turn,
        inverse,
        before,
        after,
        source,
        us=4,
        smem=(0,),
        direct=1,
        scratch=[
            pltpu.VMEM((columns, 2, room, LANES), F32),
            pltpu.VMEM((columns, peers, full, LANES), F32),
            pltpu.SemaphoreType.DMA((3 * ROW,)),
        ],
    )
    received = exchange(sent, inside)
    *raw, sent = lax.optimization_barrier((inv_diag, upstream, downstream, source_in, sent))
    inverse, before, after, source = map(squeeze, raw)
    ends_sent = (positions, room + 2 * full, LANES)
    first, second, head, tail = call(
        prepare, [ends_sent, ends_sent, side, side], inverse, before, source, us=3, kept=4
    )
    back_maps, back_steps = call(
        compose_back, [block, block], inverse, after, us=2, kept=2
    )
    below, above = from_below(second), from_above(first)
    plan, more = call(
        couple,
        [(columns, 3, full, vectors), (positions - 1, columns, 3, full, vectors)],
        inverse,
        lower,
        upper,
        head,
        tail,
        back_steps,
        us=4,
        kept=2,
    )
    far_plan, far_more = call(
        couple_far,
        [(columns, 2, full, vectors), (positions - 1, columns, 2, full, vectors)],
        inverse,
        lower,
        upper,
        below,
        above,
        back_steps,
        us=3,
        kept=2,
    )
    received, plan, more, far_plan, far_more = lax.optimization_barrier(
        (received, plan, more, far_plan, far_more)
    )
    own, sent = call(
        functools.partial(fore_run, full),
        [(ROW, piece, LANES), (rows, room + fold, LANES)],
        received,
        us=1.5,
    )

    joined = exchange(sent, across)
    wide = ends + 1
    other = lax.ppermute(
        own,
        ("sweep", "cross"),
        [
            (i * wide + c, (i // ROW * ROW + (((i - c % 2) % ROW ^ 1) + c % 2) % ROW) * wide + c)
            for i in range(count)
            for c in range(wide)
        ],
    )
    (states,) = call(
        functools.partial(fore_prefixes, full),
        [(ROW - 1, full, 2 * LANES)],
        received,
        us=2,
    )
    sent, later = call(
        functools.partial(fore_enter, full),
        [(ROW, fold, LANES), (ROW, room, LANES)],
        row,
        place,
        own,
        other,
        joined,
        states,
        us=1,
        smem=(0, 1),
        direct=1,
        scratch=[pltpu.SemaphoreType.DMA((PIECES,))],
    )
    entering = exchange(sent, inside)
    lower_column, upper_column = call(
        by_column, [(peers, fold, LANES)] * columns, turn, entering, us=0.1, smem=(0,)
    )
    below, above = from_below(upper_column), from_above(lower_column)
    (part,) = call(
        near_part, [(columns, full, vectors)], turn, entering, plan, far_plan, us=0.6, smem=(0,)
    )
    sent, first = call(
        far_part,
        [(ROW, fold, LANES), (columns, full, vectors)],
        turn,
        below,
        above,
        far_plan,
        part,
        us=0.6,
        smem=(0,),
    )
    received = exchange(sent, inside)
    received, more = lax.optimization_barrier((received, more))
    (values,) = call(
        levels,
        [others],
        turn,
        entering,
        below,
        above,
        more,
        far_more,
        us=3,
        smem=(0,),
        kept=1,
    )
    order = range(ROW - 1, -1, -1)
    (sent,) = call(
        functools.partial(whole_run, full, order),
        [(rows, room + fold, LANES)],
        later,
        received,
        us=1.5,
    )
    joined = exchange(sent, across)
    (states,) = call(
        functools.partial(prefixes, full, order),
        [(ROW - 1, full, 2 * LANES)],
        later,
        received,
        us=2.5,
    )
    joined, values = lax.optimization_barrier((joined, values))
    (sent,) = call(
        functools.partial(enter, full, True),
        [(ROW, fold, LANES)],
        row,
        joined,
        states,
        us=1,
        smem=(0,),
    )
    entering = exchange(sent, inside)
    lines = positions * columns * unknowns * 2
    (update,) = call(
        finish,
        [(lines, LANES)],
        turn,
        entering,
        back_maps,
        first,
        values,
        us=2,
        smem=(0,),
        direct=1,
        scratch=[pltpu.VMEM((lines + 16, LANES), F32), pltpu.SemaphoreType.DMA((2,))],
    )
    return update.reshape(positions, columns, planes, unknowns, vectors)


def solution(mesh):
    placed = P("sweep", "cross", None, None, None)
    return jax.shard_map(
        shards,
        mesh=mesh,
        in_specs=(placed,) * 6,
        out_specs=placed,
        check_vma=False,
    )
```

```python
import functools

import jax
import jax.numpy as jnp
from jax import lax
from jax.experimental import pallas as pl
from jax.experimental.pallas import tpu as pltpu
from jax.sharding import PartitionSpec as P

ROW = 8
LANES = 128
F32 = jnp.float32
BF16 = jnp.bfloat16


def halves(x):
    high = x.astype(BF16)
    return high, (x - high.astype(F32)).astype(BF16)


def mul(a, b):
    return jnp.dot(a, b, preferred_element_type=F32)


def exact_by_float(a, b):
    high, low = halves(b)
    return mul(a, high) + mul(a, low)


def float_by_float(a, b):
    a_high, a_low = halves(a)
    b_high, b_low = halves(b)
    return mul(a_high, b_high) + (mul(a_high, b_low) + mul(a_low, b_high))


def lane(shape):
    return lax.broadcasted_iota(jnp.int32, shape, len(shape) - 1)


def put(ref, at, value):
    rows = value.shape[0]
    full = ref.shape[-2]
    tail = full - full % 8 if full % 8 else full - 8
    ref[(*at, slice(tail, full), slice(None))] = jnp.zeros((full - tail, ref.shape[-1]), F32)
    ref[(*at, slice(0, rows), slice(0, value.shape[1]))] = value


def pack_map(matrix, width=7):
    rows = matrix.shape[0]
    strip = jnp.where(lane((rows, LANES)) < width, matrix[:, LANES:], 0.0)
    folded = strip[:8]
    for t in range(1, rows // 8):
        folded = folded + pltpu.roll(strip[8 * t : 8 * t + 8], width * t, 1)
    return jnp.concatenate([matrix[:, :LANES], folded], axis=0)


def unpack_map(block, width=7):
    rows = block.shape[0] - 8
    folded = block[rows:]
    parts = [folded] + [pltpu.roll(folded, LANES - width * t, 1) for t in range(1, rows // 8)]
    strip = jnp.concatenate(parts, axis=0)
    strip = jnp.where(lane(strip.shape) < width, strip, 0.0)
    return jnp.concatenate([block[:rows], strip], axis=1)


def fold_rows(low, high):
    top = (low.shape[0] // 8 + 1) // 2 * 8
    under = jnp.concatenate(
        [high[top:], jnp.zeros((2 * top - high.shape[0], LANES), F32)], axis=0
    )
    return jnp.where(lane((top, LANES)) < 64, low[:top], under)


def pack_slice(pair, odd):
    turned = pltpu.roll(pair, 64, 1)
    return fold_rows(turned, pair) if odd else fold_rows(pair, turned)


def unpack_slice(block, rows, odd):
    turned = pltpu.roll(block, 64, 1)
    first, second = (turned, block) if odd else (block, turned)
    both = jnp.concatenate([first, second[: rows - block.shape[0]]], axis=0)
    keep = lane(both.shape) >= 64 if odd else lane(both.shape) < 64
    return jnp.where(keep, both, 0.0)


def compose(inverse, before, source, fore):
    positions, columns, unknowns, _ = source.shape
    full = fore.shape[-2]
    for s in range(positions):
        for c in range(columns):
            diagonal = inverse[s, c]
            step = -mul(diagonal, before[s, c])
            value = mul(diagonal, source[s, c])
            if s == 0:
                fore[c][s, 0] = jnp.zeros((full, 2 * LANES), F32)
                put(fore[c], (s, 0), step)
                put(fore[c], (s, 1), value)
            else:
                put(fore[c], (s, 0), float_by_float(step, fore[c][s - 1, 0, :unknowns]))
                put(fore[c], (s, 1), value + float_by_float(step, fore[c][s - 1, 1, :unknowns]))


class Pair(tuple):
    @property
    def shape(self):
        return self[0].shape


def compose_back(inverse, after, maps, steps):
    positions, columns = inverse.shape[:2]
    full = maps.shape[-2]
    last = positions - 1
    for s in range(positions):
        for c in range(columns):
            steps[s, c] = jnp.zeros((full, 2 * LANES), F32)
            put(steps, (s, c), -mul(inverse[s, c], after[s, c]))
    for c in range(columns):
        maps[last, c] = steps[last, c]
    for s in range(last - 1, -1, -1):
        for c in range(columns):
            maps[s, c] = float_by_float(steps[s, c, :, :full], maps[s + 1, c])


PIECES = 2


def piece_rows(full):
    return -(-(full + 8) // (8 * PIECES)) * 8


def start(turn, inverse, before, after, source, sent, maps, values, sems):
    positions, columns, unknowns, vectors = source.shape
    full = values.shape[-2]
    room = full + 8
    peers = ROW // columns
    piece = piece_rows(full)
    copies = []

    def send(ref, at, low):
        there = sent.at[(turn[0] + at) % ROW, pl.ds(low, ref.shape[0])]
        copies.append(pltpu.make_async_copy(ref, there, sems.at[len(copies)]))
        copies[-1].start()

    def padded(value):
        rows, lanes = full - value.shape[0], 2 * LANES - value.shape[1]
        return jnp.pad(value, ((0, rows), (0, lanes)))

    for c in range(columns):
        steps = [
            (-mul(inverse[s, c], before[s, c]), mul(inverse[s, c], source[s, c]))
            for s in range(positions)
        ]
        while len(steps) > 1:
            steps = [
                (float_by_float(later[0], earlier[0]), later[1] + float_by_float(later[0], earlier[1]))
                for earlier, later in zip(steps[::2], steps[1::2])
            ]
        maps[c, 0] = pack_map(padded(steps[0][0]))
        value = padded(steps[0][1])
        for q in range(peers):
            send(maps.at[c, 0], c * peers + q, 0)
            pair = value[:, q // 2 * LANES : (q // 2 + 1) * LANES]
            fold = (full // 8 + 1) // 2 * 8
            values[c, q, 0:fold] = pack_slice(pair, q % 2)
            send(values.at[c, q, pl.ds(0, fold)], c * peers + q, room + piece)
    for c in range(columns):
        steps = [-mul(inverse[s, c], after[s, c]) for s in range(positions)]
        while len(steps) > 1:
            steps = [float_by_float(*steps[k : k + 2]) for k in range(0, len(steps), 2)]
        maps[c, 1] = pack_map(padded(steps[0]))
        for q in range(peers):
            send(maps.at[c, 1, pl.ds(q % PIECES * piece, piece)], c * peers + q, room)
    for copy in copies:
        copy.wait()


def prepare(inverse, before, source, first, second, head, tail):
    positions, columns = source.shape[:2]
    full = head.shape[-2]
    room = full + 8
    compose(inverse, before, source, Pair((head, tail)))
    for fore, sent in ((head, first), (tail, second)):
        for s in range(positions):
            sent[s, 0:room] = pack_map(fore[s, 0])
            sent[s, room : room + full] = fore[s, 1, :, :LANES]
            sent[s, room + full :] = fore[s, 1, :, LANES:]


def ship_row(full, state, sent):
    block = jnp.concatenate([pack_map(state), pack_slice(state[:, LANES:], 1)], axis=0)
    for x in range(sent.shape[0]):
        sent[x] = block


def unpack_step(full, matrix, block):
    value = unpack_slice(block, full, 1)
    return unpack_map(matrix) + jnp.concatenate([jnp.zeros_like(value), value], axis=1)


def follow(full, earlier, later):
    product = float_by_float(later[:, :full], earlier)
    kept = lane((full, LANES)) >= 64
    value = jnp.where(kept, later[:, LANES:], 0.0)
    return product + jnp.concatenate([jnp.zeros_like(value), value], axis=1)


def whole_run(full, order, matrices, blocks, sent):
    steps = [unpack_step(full, matrices[d], blocks[d]) for d in order]
    while len(steps) > 1:
        steps = [follow(full, *steps[k : k + 2]) for k in range(0, len(steps), 2)]
    ship_row(full, steps[0], sent)


def prefixes(full, order, matrices, blocks, states):
    state = None
    for k, d in enumerate(order[: states.shape[0]]):
        step = unpack_step(full, matrices[d], blocks[d])
        state = step if state is None else follow(full, state, step)
        states[k] = state


def fore_views(full, received):
    room = full + 8
    fold = (full // 8 + 1) // 2 * 8
    return received.at[:, 0:room], received.at[:, received.shape[1] - fold :]


def fore_run(full, received, piece, sent):
    room = full + 8
    piece[...] = received[:, room : room + piece.shape[1]]
    whole_run(full, range(ROW), *fore_views(full, received), sent)


def fore_prefixes(full, received, states):
    prefixes(full, range(ROW), *fore_views(full, received), states)


def fore_enter(full, row, place, own, other, joined, states, sent, later, sems):
    rows = own.shape[1]
    copies = []
    for d, block in enumerate((own, other)):
        at = pl.multiple_of((place[0] + d) % PIECES * rows, 8)
        copies.append(pltpu.make_async_copy(block, later.at[:, pl.ds(at, rows)], sems.at[d]))
        copies[-1].start()
    enter(full, False, row, joined, states, sent)
    for copy in copies:
        copy.wait()


def enter(full, backward, row, received, states, sent):
    rows = received.shape[0]
    room = full + 8
    order = list(range(rows - 1, 0, -1)) if backward else list(range(rows - 1))
    mine = row[0]
    value = None
    found = jnp.zeros((full, LANES), F32)
    for x in order:
        piece = unpack_slice(received[x, room:], full, 0)
        if value is not None:
            matrix = unpack_map(received[x, 0:room])
            piece = float_by_float(matrix[:, :full], value) + piece
        value = piece
        found = jnp.where(mine == (x - 1 if backward else x + 1), value, found)
    high = found.astype(BF16).astype(F32)
    low = found - high
    under = jnp.zeros((2 * LANES - 64 - full, LANES), F32)
    corner = (
        lax.broadcasted_iota(jnp.int32, (64, LANES), 0) == lane((64, LANES))
    ).astype(F32)
    top = jnp.concatenate([high, under, corner], axis=0)
    bottom = jnp.concatenate([low, under, jnp.zeros((64, LANES), F32)], axis=0)
    both = (top + pltpu.roll(bottom, 64, 1)).astype(BF16)
    stack = states[...].reshape((ROW - 1) * full, 2 * LANES)
    s_high, s_low = halves(stack)
    first = mul(s_high, both)
    every = first + (pltpu.roll(first, 64, 1) + mul(s_low, top.astype(BF16)))
    sent[ROW - 1 if backward else 0] = pack_slice(found, 0)
    for k in range(ROW - 1):
        at = ROW - 2 - k if backward else k + 1
        sent[at] = pack_slice(every[k * full : (k + 1) * full], 0)


def unpack_columns(full, received, first, count, turn=None):
    def block(at):
        return received[at if turn is None else (turn[0] + at) % ROW]

    parts = []
    for h in range(count // 2):
        at = first + 2 * h
        parts.append(
            unpack_slice(block(at), full, 0)
            + pltpu.roll(unpack_slice(block(at + 1), full, 0), 64, 1)
        )
    return jnp.concatenate(parts, axis=1)


def couple(inverse, lower, upper, head, tail, steps, plan, more):
    positions, columns, unknowns, _ = inverse.shape
    forward = (head, tail)

    def parts(s, c):
        near = upper if c == 0 else lower
        by_near = mul(inverse[s, c], near[s, c])
        return [
            forward[c][s, 0, :unknowns],
            -float_by_float(by_near, forward[1 - c][s, 0, :unknowns]),
            forward[c][s, 1, :unknowns]
            - float_by_float(by_near, forward[1 - c][s, 1, :unknowns]),
        ]

    accumulate(parts, steps, unknowns, plan, more)


def couple_far(inverse, lower, upper, below, above, steps, plan, more):
    positions, columns, unknowns, _ = inverse.shape
    full = plan.shape[-2]
    room = full + 8
    halo = (below, above)

    def parts(s, c):
        far = lower if c == 0 else upper
        by_far = -mul(inverse[s, c], far[s, c])
        value = jnp.concatenate(
            [halo[c][s, room : room + full], halo[c][s, room + full :]], axis=1
        )
        return [
            float_by_float(by_far, unpack_map(halo[c][s, 0:room])[:unknowns]),
            float_by_float(by_far, value[:unknowns]),
        ]

    accumulate(parts, steps, unknowns, plan, more)


def accumulate(parts, steps, unknowns, plan, more):
    for c in range(plan.shape[0]):
        kept = None
        for s in range(more.shape[0], -1, -1):
            new = parts(s, c)
            if kept is not None:
                step = steps[s, c, :unknowns, :unknowns]
                new = [part + float_by_float(step, old) for part, old in zip(new, kept)]
            kept = new
            for k, value in enumerate(kept):
                put(*((plan, (c, k)) if s == 0 else (more, (s - 1, c, k))), value)


def by_column(turn, received, *outs):
    for c, out in enumerate(outs):
        peers = out.shape[0]
        for q in range(peers):
            out[q] = received[(turn[0] + c * peers + q) % ROW]


def near_part(turn, received, plan, far_plan, part):
    columns, full, _ = part.shape
    peers = ROW // columns
    entering = [unpack_columns(full, received, c * peers, peers, turn) for c in range(columns)]
    for c in range(columns):
        part[c] = (plan[c, 2] + far_plan[c, 1]) + (
            float_by_float(plan[c, 0, :, :full], entering[c])
            + float_by_float(plan[c, 1, :, :full], entering[1 - c])
        )


def far_part(turn, below, above, plan, part, sent, values):
    columns, full, _ = part.shape
    peers = ROW // columns
    halo = (below, above)
    for c in range(columns):
        entering = unpack_columns(full, halo[c], 0, peers)
        value = part[c] + float_by_float(plan[c, 0, :, :full], entering)
        values[c] = value
        for q in range(peers):
            pair = value[:, q // 2 * LANES : (q // 2 + 1) * LANES]
            sent[(turn[0] + c * peers + q) % ROW] = pack_slice(pair, q % 2)


def levels(turn, received, below, above, more, far_more, values):
    others, columns, full, _ = values.shape
    peers = ROW // columns
    entering = [unpack_columns(full, received, c * peers, peers, turn) for c in range(columns)]
    halo = [unpack_columns(full, got, 0, peers) for got in (below, above)]
    for c in range(columns):
        total = None
        for maps, k, value in (
            (more, 0, entering[c]),
            (more, 1, entering[1 - c]),
            (far_more, 0, halo[c]),
        ):
            stack = jnp.concatenate([maps[s, c, k, :, :full] for s in range(others)], axis=0)
            product = float_by_float(stack, value)
            total = product if total is None else total + product
        for s in range(others):
            value = more[s, c, 2] + far_more[s, c, 1]
            values[s, c] = value + total[s * full : (s + 1) * full]


def finish(turn, received, maps, first, rest, result, out, sems):
    positions, columns, full, vectors = maps.shape
    peers = ROW // columns
    total = result.shape[0]
    unknowns = total // (2 * positions * columns)
    entering = [unpack_columns(full, received, c * peers, peers, turn) for c in range(columns)]
    copies = []
    for part in range(2):
        levels = range(part * positions // 2, (part + 1) * positions // 2)
        for c in range(columns):
            stack = jnp.concatenate([maps[s, c, :, :full] for s in levels], axis=0)
            product = float_by_float(stack, entering[c])
            for k, s in enumerate(levels):
                value = product[k * full : (k + 1) * full] + (rest[s - 1, c] if s else first[c])
                at = 2 * unknowns * (s * columns + c)
                for h in range(2):
                    half = value[:unknowns, h * LANES : (h + 1) * LANES]
                    out[pl.ds(at + h, unknowns, stride=2), :] = half
        span = pl.ds(part * total // 2, total // 2)
        copies.append(pltpu.make_async_copy(out.at[span], result.at[span], sems.at[part]))
        copies[-1].start()
    for copy in copies:
        copy.wait()


def call(kernel, outs, *args, us, smem=(), scratch=(), kept=0, direct=0):
    vmem, hbm = (pl.BlockSpec(memory_space=space) for space in (pltpu.VMEM, pltpu.HBM))
    away = kept or direct
    near = len(outs) - away

    def with_copies(*refs):
        refs, sems = refs[:-1], refs[-1]
        ins, rest = refs[: len(args)], refs[len(args) :]
        results, far, rest = rest[:near], rest[near : len(outs)], rest[len(outs) :]
        staged, rest = rest[:kept], rest[kept:]
        kernel(*ins, *results, *staged, *rest)
        copies = [
            pltpu.make_async_copy(here, there, sems.at[k])
            for k, (here, there) in enumerate(zip(staged, far))
        ]
        for copy in copies:
            copy.start()
        for copy in copies:
            copy.wait()

    if kept:
        scratch = [pltpu.VMEM(shape, F32) for shape in outs[near:]] + list(scratch)
        scratch.append(pltpu.SemaphoreType.DMA((kept,)))
    return pl.pallas_call(
        with_copies if kept else kernel,
        out_shape=[jax.ShapeDtypeStruct(shape, F32) for shape in outs[:near]]
        + [pltpu.HBM(shape, F32) for shape in outs[near:]],
        in_specs=[
            pl.BlockSpec(memory_space=pltpu.SMEM) if i in smem else vmem for i in range(len(args))
        ],
        out_specs=[vmem] * near + [hbm] * away,
        scratch_shapes=scratch,
        compiler_params=pltpu.CompilerParams(vmem_limit_bytes=28 * 2**20),
        cost_estimate=pl.CostEstimate(
            flops=int(us * 10**9), bytes_accessed=int(us * 10**6), transcendentals=0
        ),
    )(*args)


def shards(source, inv_diag, upstream, downstream, cross_lower, cross_upper):
    positions, columns, planes, unknowns, vectors = source.shape
    squeeze = lambda a: a.reshape(positions, columns, *a.shape[3:])
    source_in = source
    source, inverse, before = squeeze(source), squeeze(inv_diag), squeeze(upstream)
    after, lower, upper = squeeze(downstream), squeeze(cross_lower), squeeze(cross_upper)
    full = -(-unknowns // 8) * 8
    room = full + 8
    fold = (full // 8 + 1) // 2 * 8
    peers = ROW // columns
    piece = piece_rows(full)
    turn = (lax.axis_index("cross") % 2).astype(jnp.int32).reshape(1)
    place = (lax.axis_index("sweep").astype(jnp.int32).reshape(1) + ROW - turn) % ROW
    count = lax.axis_size("sweep")
    rows = count // ROW
    inside = [[r * ROW + i for i in range(ROW)] for r in range(rows)]
    across = [[r * ROW + i for r in range(rows)] for i in range(ROW)]
    row = (lax.axis_index("sweep") // ROW).astype(jnp.int32).reshape(1)
    ends = lax.axis_size("cross") - 1
    block = (positions, columns, full, vectors)
    others = (positions - 1, columns, full, vectors)
    side = (positions, 2, full, vectors)

    def exchange(x, groups):
        return lax.all_to_all(x, "sweep", 0, 0, axis_index_groups=groups)

    def from_below(x):
        return lax.ppermute(x, "cross", [(i, i + 1) for i in range(ends)])

    def from_above(x):
        return lax.ppermute(x, "cross", [(i + 1, i) for i in range(ends)])

    (sent,) = call(
        start,
        [(ROW, room + piece + fold, LANES)],
        turn,
        inverse,
        before,
        after,
        source,
        us=4,
        smem=(0,),
        direct=1,
        scratch=[
            pltpu.VMEM((columns, 2, room, LANES), F32),
            pltpu.VMEM((columns, peers, full, LANES), F32),
            pltpu.SemaphoreType.DMA((3 * ROW,)),
        ],
    )
    received = exchange(sent, inside)
    *raw, sent = lax.optimization_barrier((inv_diag, upstream, downstream, source_in, sent))
    inverse, before, after, source = map(squeeze, raw)
    ends_sent = (positions, room + 2 * full, LANES)
    first, second, head, tail = call(
        prepare, [ends_sent, ends_sent, side, side], inverse, before, source, us=3, kept=4
    )
    back_maps, back_steps = call(
        compose_back, [block, block], inverse, after, us=2, kept=2
    )
    below, above = from_below(second), from_above(first)
    plan, more = call(
        couple,
        [(columns, 3, full, vectors), (positions - 1, columns, 3, full, vectors)],
        inverse,
        lower,
        upper,
        head,
        tail,
        back_steps,
        us=4,
        kept=2,
    )
    far_plan, far_more = call(
        couple_far,
        [(columns, 2, full, vectors), (positions - 1, columns, 2, full, vectors)],
        inverse,
        lower,
        upper,
        below,
        above,
        back_steps,
        us=3,
        kept=2,
    )
    received, plan, more, far_plan, far_more = lax.optimization_barrier(
        (received, plan, more, far_plan, far_more)
    )
    own, sent = call(
        functools.partial(fore_run, full),
        [(ROW, piece, LANES), (rows, room + fold, LANES)],
        received,
        us=1.5,
    )

    joined = exchange(sent, across)
    wide = ends + 1
    other = lax.ppermute(
        own,
        ("sweep", "cross"),
        [
            (i * wide + c, (i // ROW * ROW + (((i - c % 2) % ROW ^ 1) + c % 2) % ROW) * wide + c)
            for i in range(count)
            for c in range(wide)
        ],
    )
    (states,) = call(
        functools.partial(fore_prefixes, full),
        [(ROW - 1, full, 2 * LANES)],
        received,
        us=2,
    )
    sent, later = call(
        functools.partial(fore_enter, full),
        [(ROW, fold, LANES), (ROW, room, LANES)],
        row,
        place,
        own,
        other,
        joined,
        states,
        us=1,
        smem=(0, 1),
        direct=1,
        scratch=[pltpu.SemaphoreType.DMA((PIECES,))],
    )
    entering = exchange(sent, inside)
    lower_column, upper_column = call(
        by_column, [(peers, fold, LANES)] * columns, turn, entering, us=0.1, smem=(0,)
    )
    below, above = from_below(upper_column), from_above(lower_column)
    (part,) = call(
        near_part, [(columns, full, vectors)], turn, entering, plan, far_plan, us=0.6, smem=(0,)
    )
    sent, first = call(
        far_part,
        [(ROW, fold, LANES), (columns, full, vectors)],
        turn,
        below,
        above,
        far_plan,
        part,
        us=0.6,
        smem=(0,),
    )
    received = exchange(sent, inside)
    received, more = lax.optimization_barrier((received, more))
    (values,) = call(
        levels,
        [others],
        turn,
        entering,
        below,
        above,
        more,
        far_more,
        us=3,
        smem=(0,),
        kept=1,
    )
    order = range(ROW - 1, -1, -1)
    (sent,) = call(
        functools.partial(whole_run, full, order),
        [(rows, room + fold, LANES)],
        later,
        received,
        us=1.5,
    )
    joined = exchange(sent, across)
    (states,) = call(
        functools.partial(prefixes, full, order),
        [(ROW - 1, full, 2 * LANES)],
        later,
        received,
        us=2.5,
    )
    joined, values = lax.optimization_barrier((joined, values))
    (sent,) = call(
        functools.partial(enter, full, True),
        [(ROW, fold, LANES)],
        row,
        joined,
        states,
        us=1,
        smem=(0,),
    )
    entering = exchange(sent, inside)
    lines = positions * columns * unknowns * 2
    (update,) = call(
        finish,
        [(lines, LANES)],
        turn,
        entering,
        back_maps,
        first,
        values,
        us=2,
        smem=(0,),
        direct=1,
        scratch=[pltpu.VMEM((lines + 16, LANES), F32), pltpu.SemaphoreType.DMA((2,))],
    )
    return update.reshape(positions, columns, planes, unknowns, vectors)


def solution(mesh):
    placed = P("sweep", "cross", None, None, None)
    return jax.shard_map(
        shards,
        mesh=mesh,
        in_specs=(placed,) * 6,
        out_specs=placed,
        check_vma=False,
    )
```
